32 devices in a mesh: groups: 1, seq: 32 (over z, y, x, core), dp: 1.
Axes of the slice: x: 2, y: 2, z: 4, core: 2. Of those that a mesh axis runs over, the one named last changes fastest.
Arguments:
- values: bfloat16 [1, 256, 256, 768], P(('groups', 'dp'), 'seq'), may hold values from -6 to 6
- kernel: bfloat16 [256, 256, 768], P('seq'), may hold values from -6 to 6
- cotangent: bfloat16 [1, 256, 256, 768], P(('groups', 'dp'), 'seq'), may hold values from -6 to 6
- inner_factor: bfloat16 [256, 256], replicated, may hold values from -0.375 to 0.375
- outer_factor: bfloat16 [256, 256], replicated, may hold values from -0.375 to 0.375
- return_outer: bfloat16 [256, 256], replicated, may hold values from -0.375 to 0.375
- return_inner: bfloat16 [256, 256], replicated, may hold values from -0.375 to 0.375
Outputs:
- grad_values: bfloat16 [1, 256, 256, 768], P(('groups', 'dp'), 'seq')
- grad_inner: float32 [256, 256], P('groups')
- grad_outer: float32 [256, 256], P('groups')
- grad_return_outer: float32 [256, 256], P('groups')
- grad_return_inner: float32 [256, 256], P('groups')
The draws below stay inside these ranges and needn't reach their ends.
All inputs are finite; a program needn't handle non-finite values.
Results may differ from the reference program's by a relative error of at most 0.0064.
Values may be sent and summed in bfloat16 or wider, within the bound.
No kernel may reach another device: no remote copies, remote signals or barrier semaphores. Data moves between devices by JAX's collectives and lax.ppermute only.
A program may use at most 64 MiB of HBM per device.

```python
import math
import jax
import jax.numpy as jnp
from jax import lax

NA = 256
NB = 256
C = 768
SEQS = 1


def block_levels(own_key, dims, shards, least, high):
    level, own = 1.0, jax.random.fold_in(own_key, 6)
    for dim, parts in shards:
        draws = jnp.exp(jax.random.uniform(jax.random.fold_in(own, dim), (parts,), jnp.float32, least / len(shards), high / len(shards)))
        level = level * jnp.repeat(draws, dims[dim] // parts).reshape([-1 if axis == dim else 1 for axis in range(len(dims))])
    return level


def noise(key, extent, width, limit, pieces=(), dtype=jnp.bfloat16):
    array = width * jax.random.normal(key, extent, jnp.float32)
    if pieces:
        array = array * block_levels(key, extent, pieces, -0.22, 0.18)
    return jnp.clip(array, -limit, limit).astype(dtype)


def setup_inputs(seed: int = 0, part: int = 0) -> dict:
    streams_of = jax.random.split(jax.random.key(seed), 8)
    part_keys = jax.random.split(jax.random.fold_in(streams_of[7], part), 8)
    return {
        "values": noise(part_keys[0], (SEQS, NA, NB, C), 1.0, 6.0, ((1, 32),)),
        "kernel": noise(streams_of[1], (NB, NA, C), 1.0, 6.0, ((0, 32),)),
        "cotangent": noise(part_keys[2], (SEQS, NA, NB, C), 1.0, 6.0, ((1, 32),)),
        "inner_factor": noise(streams_of[3], (NB, NB), NB ** -0.5, 0.375),
        "outer_factor": noise(streams_of[4], (NA, NA), NA ** -0.5, 0.375),
        "return_outer": noise(streams_of[5], (NA, NA), NA ** -0.5, 0.375),
        "return_inner": noise(streams_of[6], (NB, NB), NB ** -0.5, 0.375),
    }


def reference(values, kernel, cotangent, inner_factor, outer_factor, return_outer, return_inner):
    kern = kernel.astype(jnp.float32)
    fone = inner_factor.astype(jnp.float32)
    ftwo = outer_factor.astype(jnp.float32)
    gone = return_outer.astype(jnp.float32)
    gtwo = return_inner.astype(jnp.float32)

    def one_sequence(inputs):
        source, grad_out = inputs
        source = source.astype(jnp.float32)
        grad_out = grad_out.astype(jnp.float32)
        first = jnp.einsum('jb,abc->ajc', fone, source).astype(jnp.bfloat16).astype(jnp.float32)
        weighted = (jnp.einsum('ia,ajc->jic', ftwo, first) * kern).astype(jnp.bfloat16).astype(jnp.float32)
        returned = jnp.einsum('ki,jic->kjc', gone, weighted).astype(jnp.bfloat16).astype(jnp.float32)
        grad_returned = jnp.einsum('lj,klc->kjc', gtwo, grad_out).astype(jnp.bfloat16).astype(jnp.float32)
        grad_gtwo = jnp.einsum('klc,kjc->lj', grad_out, returned)
        grad_weighted = (jnp.einsum('ki,kjc->jic', gone, grad_returned) * kern).astype(jnp.bfloat16).astype(jnp.float32)
        grad_gone = jnp.einsum('kjc,jic->ki', grad_returned, weighted)
        grad_first = jnp.einsum('ia,jic->ajc', ftwo, grad_weighted).astype(jnp.bfloat16).astype(jnp.float32)
        grad_ftwo = jnp.einsum('jic,ajc->ia', grad_weighted, first)
        grad_source = jnp.einsum('jb,ajc->abc', fone, grad_first).astype(jnp.bfloat16)
        grad_fone = jnp.einsum('ajc,abc->jb', grad_first, source)
        return (grad_source, (grad_fone, grad_ftwo, grad_gone, grad_gtwo))
    grad_values, stacked = lax.map(one_sequence, (values, cotangent))
    scale_a = 1.0 / math.sqrt(SEQS * NA * C)
    scale_b = 1.0 / math.sqrt(SEQS * NB * C)
    grad_inner = lax.optimization_barrier(jnp.sum(stacked[0], axis=0)) * scale_a
    grad_outer = lax.optimization_barrier(jnp.sum(stacked[1], axis=0)) * scale_b
    grad_return_outer = lax.optimization_barrier(jnp.sum(stacked[2], axis=0)) * scale_b
    grad_return_inner = lax.optimization_barrier(jnp.sum(stacked[3], axis=0)) * scale_a
    return (grad_values, grad_inner, grad_outer, grad_return_outer, grad_return_inner)
```

```python
import math

import jax
import jax.numpy as jnp
from jax import lax
from jax.experimental import pallas as pl
from jax.experimental.pallas import tpu as pltpu
from jax.sharding import PartitionSpec as P

F32 = jnp.float32
BF16 = jnp.bfloat16
LANES = 128
VMEM = 56 * 2**20


def dot(x, y, dims):
    return lax.dot_general(x, y, ((dims[:1], dims[1:]), ((), ())), preferred_element_type=F32)


def call(body, grid, ins, outs, scratch, flops, moved):
    return pl.pallas_call(
        body,
        grid=grid,
        in_specs=[spec for spec in ins],
        out_specs=[spec for spec, _ in outs],
        out_shape=[shape for _, shape in outs],
        scratch_shapes=scratch,
        compiler_params=pltpu.CompilerParams(
            vmem_limit_bytes=VMEM, dimension_semantics=("arbitrary",) * len(grid)
        ),
        cost_estimate=pl.CostEstimate(flops=flops, bytes_accessed=moved, transcendentals=0),
    )


def square(order):
    return pl.BlockSpec((order, order), lambda *g: (0, 0))


def apply_inner(x, factor, side, members):
    rows, order, channels = x.shape
    part = order // members
    step = max(1, rows // 4)

    def body(x_ref, f_ref, o_ref):
        for r in range(step):
            y = dot(f_ref[...], x_ref[r], (side, 0))
            o_ref[:, r] = y.reshape(members, part, channels).astype(BF16)

    return call(
        body,
        (rows // step,),
        [pl.BlockSpec((step, order, channels), lambda g: (g, 0, 0)), square(order)],
        [
            (
                pl.BlockSpec((members, step, part, channels), lambda g: (0, g, 0, 0)),
                jax.ShapeDtypeStruct((members, rows, part, channels), BF16),
            )
        ],
        [],
        2 * order * x.size,
        4 * x.size,
    )(x, factor)[0]


def tile_pairs(part, width):
    tiles = [(j, t) for j in range(part) for t in range(width // LANES)]
    return [tiles[p : p + 2] for p in range(0, len(tiles), 2)]


def spread(ref, value):
    order, part, width = value.shape
    for t in range(width // LANES):
        ref[t] = value[:, :, t * LANES : (t + 1) * LANES].astype(F32).reshape(order * part, LANES)


def take(ref, pair, order, part):
    got = [ref[t, pl.ds(j, order, stride=part), :] for j, t in pair]
    return jnp.concatenate(got, axis=1).astype(BF16)


def put(ref, pair, order, part, value):
    for n, (j, t) in enumerate(pair):
        ref[t, pl.ds(j, order, stride=part), :] = value[:, n * LANES : (n + 1) * LANES]


def gather(ref, members, part):
    tiles = [ref[t].reshape(members, -1, part, LANES).astype(BF16) for t in range(ref.shape[0])]
    return jnp.concatenate(tiles, axis=-1)


def pick(ref, pair):
    return jnp.concatenate([ref[j, :, t * LANES : (t + 1) * LANES] for j, t in pair], axis=1)


def backward_mixed(moved, kernel, outer, back, members):
    order, part, channels = moved.shape
    width = min(channels, 2 * LANES)
    local = order // members

    def body(m_ref, k_ref, o_ref, b_ref, gw_ref, gf_ref, held, result):
        spread(held, m_ref[...])
        for pair in tile_pairs(part, width):
            mixed = dot(b_ref[...], take(held, pair, order, part), (0, 0))
            gw = (mixed * pick(k_ref, pair).astype(F32)).astype(BF16)
            for n, (j, t) in enumerate(pair):
                gw_ref[j, :, t * LANES : (t + 1) * LANES] = gw[:, n * LANES : (n + 1) * LANES]
            put(result, pair, order, part, dot(o_ref[...], gw, (0, 0)))
        gf_ref[...] = gather(result, members, part)

    return call(
        body,
        (channels // width,),
        [
            pl.BlockSpec((order, part, width), lambda g: (0, 0, g)),
            pl.BlockSpec((part, order, width), lambda g: (0, 0, g)),
            square(order),
            square(order),
        ],
        [
            (
                pl.BlockSpec((part, order, width), lambda g: (0, 0, g)),
                jax.ShapeDtypeStruct((part, order, channels), BF16),
            ),
            (
                pl.BlockSpec((members, local, part, width), lambda g: (0, 0, 0, g)),
                jax.ShapeDtypeStruct((members, local, part, channels), BF16),
            ),
        ],
        [pltpu.VMEM((width // LANES, order * part, LANES), F32)] * 2,
        4 * order * moved.size,
        8 * moved.size,
    )(moved, kernel, outer, back)


def forward_mixed(first, grad_ret, kernel, gw, outer, back, members):
    order, part, channels = first.shape
    width = min(channels, 2 * LANES)
    local = order // members

    def body(f_ref, g_ref, k_ref, gw_ref, o_ref, b_ref, ret_ref, go_ref, gr_ref, held, held_g, result):
        @pl.when(pl.program_id(0) == 0)
        def _():
            go_ref[...] = jnp.zeros_like(go_ref)
            gr_ref[...] = jnp.zeros_like(gr_ref)

        spread(held, f_ref[...])
        spread(held_g, g_ref[...])
        for pair in tile_pairs(part, width):
            first_j = take(held, pair, order, part)
            mixed = dot(o_ref[...], first_j, (1, 0))
            weighted = (mixed * pick(k_ref, pair).astype(F32)).astype(BF16)
            put(result, pair, order, part, dot(b_ref[...], weighted, (1, 0)))
            go_ref[...] += dot(pick(gw_ref, pair), first_j, (1, 1))
            gr_ref[...] += dot(take(held_g, pair, order, part), weighted, (1, 1))
        ret_ref[...] = gather(result, members, part)

    moved = pl.BlockSpec((order, part, width), lambda g: (0, 0, g))
    mine = pl.BlockSpec((part, order, width), lambda g: (0, 0, g))
    small = (square(order), jax.ShapeDtypeStruct((order, order), F32))
    return call(
        body,
        (channels // width,),
        [moved, moved, mine, mine, square(order), square(order)],
        [
            (
                pl.BlockSpec((members, local, part, width), lambda g: (0, 0, 0, g)),
                jax.ShapeDtypeStruct((members, local, part, channels), BF16),
            ),
            small,
            small,
        ],
        [pltpu.VMEM((width // LANES, order * part, LANES), F32)] * 3,
        8 * order * first.size,
        10 * first.size,
    )(first, grad_ret, kernel, gw, outer, back)


def finish_values(grad_first, values, inner):
    members, rows, part, channels = grad_first.shape
    order = members * part
    step = max(1, rows // 4)

    def body(g_ref, v_ref, f_ref, gv_ref, gi_ref):
        @pl.when(pl.program_id(0) == 0)
        def _():
            gi_ref[...] = jnp.zeros_like(gi_ref)

        for r in range(step):
            g = g_ref[:, r].astype(F32).reshape(order, channels).astype(BF16)
            gv_ref[r] = dot(f_ref[...], g, (0, 0)).astype(BF16)
            gi_ref[...] += dot(g, v_ref[r], (1, 1))

    rowed = pl.BlockSpec((step, order, channels), lambda g: (g, 0, 0))
    return call(
        body,
        (rows // step,),
        [pl.BlockSpec((members, step, part, channels), lambda g: (0, g, 0, 0)), rowed, square(order)],
        [
            (rowed, jax.ShapeDtypeStruct(values.shape, BF16)),
            (square(order), jax.ShapeDtypeStruct((order, order), F32)),
        ],
        [],
        4 * order * values.size,
        6 * values.size,
    )(grad_first, values, inner)


def finish_return(returned, cotangent):
    members, rows, part, channels = returned.shape
    order = members * part
    step = max(1, rows // 4)

    def body(r_ref, c_ref, o_ref):
        @pl.when(pl.program_id(0) == 0)
        def _():
            o_ref[...] = jnp.zeros_like(o_ref)

        for r in range(step):
            ret = r_ref[:, r].astype(F32).reshape(order, channels).astype(BF16)
            o_ref[...] += dot(c_ref[r], ret, (1, 1))

    return call(
        body,
        (rows // step,),
        [
            pl.BlockSpec((members, step, part, channels), lambda g: (0, g, 0, 0)),
            pl.BlockSpec((step, order, channels), lambda g: (g, 0, 0)),
        ],
        [(square(order), jax.ShapeDtypeStruct((order, order), F32))],
        [],
        2 * order * cotangent.size,
        4 * cotangent.size,
    )(returned, cotangent)[0]


def plain(values, kernel, cotangent, inner_factor, outer_factor, return_outer, return_inner):
    f32 = F32
    bf16 = BF16
    order_a = outer_factor.shape[0]
    order_b = inner_factor.shape[0]
    channels = kernel.shape[2]
    seq_count = values.shape[0] * lax.axis_size("dp")
    scale_a = 1.0 / math.sqrt(seq_count * order_a * channels)
    scale_b = 1.0 / math.sqrt(seq_count * order_b * channels)
    first = jnp.einsum("jb,sabc->sajc", inner_factor, values, preferred_element_type=f32).astype(
        bf16
    )
    piece = lax.all_to_all(first, "seq", split_axis=2, concat_axis=1, tiled=True)
    mixed = jnp.einsum("ia,sajc->sjic", outer_factor, piece, preferred_element_type=f32)
    first_moved = piece
    weighted = (mixed * kernel[None].astype(f32)).astype(bf16)
    returned_local = jnp.einsum(
        "ki,sjic->sjkc", return_outer, weighted, preferred_element_type=f32
    ).astype(bf16)
    returned = lax.all_to_all(returned_local, "seq", split_axis=2, concat_axis=1, tiled=True)
    grad_returned = jnp.einsum(
        "lj,sklc->skjc", return_inner, cotangent, preferred_element_type=f32
    ).astype(bf16)
    grad_gtwo = jnp.einsum("sklc,sjkc->lj", cotangent, returned, preferred_element_type=f32)
    piece = lax.all_to_all(grad_returned, "seq", split_axis=2, concat_axis=1, tiled=True)
    grad_mixed = jnp.einsum("ki,skjc->sjic", return_outer, piece, preferred_element_type=f32)
    grad_ret_moved = piece
    grad_gone = jnp.einsum("skjc,sjic->ki", grad_ret_moved, weighted, preferred_element_type=f32)
    grad_weighted = (grad_mixed * kernel[None].astype(f32)).astype(bf16)
    grad_first_moved = jnp.einsum(
        "ia,sjic->sajc", outer_factor, grad_weighted, preferred_element_type=f32
    ).astype(bf16)
    grad_ftwo = jnp.einsum("sjic,sajc->ia", grad_weighted, first_moved, preferred_element_type=f32)
    piece = lax.all_to_all(grad_first_moved, "seq", split_axis=1, concat_axis=2, tiled=True)
    grad_values = jnp.einsum(
        "jb,sajc->sabc", inner_factor, piece, preferred_element_type=f32
    ).astype(bf16)
    grad_fone = jnp.einsum("sajc,sabc->jb", piece, values, preferred_element_type=f32)
    summed = lax.psum((grad_fone, grad_ftwo, grad_gone, grad_gtwo), ("seq", "dp"))
    return (
        grad_values,
        summed[0] * scale_a,
        summed[1] * scale_b,
        summed[2] * scale_b,
        summed[3] * scale_a,
    )


def swap(x, bit):
    size = lax.axis_size("seq")
    return lax.ppermute(x, "seq", [(i, i ^ bit) for i in range(size)])


def total(x):
    size = lax.axis_size("seq")
    plane = [[z * 8 + p for p in range(8)] for z in range(size // 8)]
    rows, columns = x.shape
    parts = lax.all_to_all(
        x.astype(BF16).reshape(8, rows // 8, columns), "seq", 0, 0, axis_index_groups=plane, tiled=True
    )
    held = jnp.sum(parts.astype(F32), axis=0).astype(BF16)
    sent = sum(swap(held, 8 * d).astype(F32) for d in (2,)) + held.astype(F32)
    sent = sent.astype(BF16)
    part = sent.astype(F32) + swap(sent, 8).astype(F32)
    out = jnp.broadcast_to(part.astype(BF16)[None], (8, rows // 8, columns))
    return lax.all_to_all(out, "seq", 0, 0, axis_index_groups=plane, tiled=True).reshape(rows, columns)


def per_device(values, kernel, cotangent, inner_factor, outer_factor, return_outer, return_inner):
    members = lax.axis_size("seq")
    order = outer_factor.shape[0]
    rows, channels = kernel.shape[0], kernel.shape[2]
    if (
        members != 32
        or lax.axis_size("dp") != 1
        or values.shape[0] != 1
        or rows != 8
        or inner_factor.shape[0] != order
        or channels % (2 * LANES)
    ):
        return plain(
            values, kernel, cotangent, inner_factor, outer_factor, return_outer, return_inner
        )
    scale = 1.0 / math.sqrt(order * channels)

    def move(x):
        return lax.all_to_all(x, "seq", 0, 0, tiled=True)

    grad_ret = move(apply_inner(cotangent[0], return_inner, 0, members))
    sent = apply_inner(values[0], inner_factor, 1, members)
    sent, grad_ret = lax.optimization_barrier((sent, grad_ret))
    first = move(sent)
    grad_ret = grad_ret.reshape(order, rows, channels)
    gw, sent = backward_mixed(grad_ret, kernel, outer_factor, return_outer, members)
    sent, first = lax.optimization_barrier((sent, first))
    grad_first = move(sent)
    first = first.reshape(order, rows, channels)
    sent, grad_outer, grad_back = forward_mixed(
        first, grad_ret, kernel, gw, outer_factor, return_outer, members
    )
    sent, grad_first = lax.optimization_barrier((sent, grad_first))
    returned = move(sent)
    grad_values, grad_inner = finish_values(grad_first, values[0], inner_factor)
    grad_last = finish_return(returned, cotangent[0])
    grads = total(jnp.concatenate((grad_inner, grad_outer, grad_back, grad_last), axis=1))
    grads = jnp.split(grads.astype(F32) * scale, 4, axis=1)
    return (grad_values[None], *grads)


def solution(mesh):
    return jax.shard_map(
        per_device,
        mesh=mesh,
        in_specs=(
            P(("groups", "dp"), "seq", None, None),
            P("seq", None, None),
            P(("groups", "dp"), "seq", None, None),
            P(),
            P(),
            P(),
            P(),
        ),
        out_specs=(
            P(("groups", "dp"), "seq", None, None),
            P("groups", None),
            P("groups", None),
            P("groups", None),
            P("groups", None),
        ),
        check_vma=False,
    )
```

```python
import math

import jax
import jax.numpy as jnp
from jax import lax
from jax.experimental import pallas as pl
from jax.experimental.pallas import tpu as pltpu
from jax.sharding import PartitionSpec as P

F32 = jnp.float32
BF16 = jnp.bfloat16
LANES = 128
VMEM = 56 * 2**20


def dot(x, y, dims):
    return lax.dot_general(x, y, ((dims[:1], dims[1:]), ((), ())), preferred_element_type=F32)


def call(body, grid, ins, outs, scratch, flops, moved):
    return pl.pallas_call(
        body,
        grid=grid,
        in_specs=[spec for spec in ins],
        out_specs=[spec for spec, _ in outs],
        out_shape=[shape for _, shape in outs],
        scratch_shapes=scratch,
        compiler_params=pltpu.CompilerParams(
            vmem_limit_bytes=VMEM, dimension_semantics=("arbitrary",) * len(grid)
        ),
        cost_estimate=pl.CostEstimate(flops=flops, bytes_accessed=moved, transcendentals=0),
    )


def square(order):
    return pl.BlockSpec((order, order), lambda *g: (0, 0))


def apply_inner(x, factor, side, members):
    rows, order, channels = x.shape
    part = order // members
    step = max(1, rows // 4)

    def body(x_ref, f_ref, o_ref):
        for r in range(step):
            y = dot(f_ref[...], x_ref[r], (side, 0))
            o_ref[:, r] = y.reshape(members, part, channels).astype(BF16)

    return call(
        body,
        (rows // step,),
        [pl.BlockSpec((step, order, channels), lambda g: (g, 0, 0)), square(order)],
        [
            (
                pl.BlockSpec((members, step, part, channels), lambda g: (0, g, 0, 0)),
                jax.ShapeDtypeStruct((members, rows, part, channels), BF16),
            )
        ],
        [],
        2 * order * x.size,
        4 * x.size,
    )(x, factor)[0]


def tile_pairs(part, width):
    tiles = [(j, t) for j in range(part) for t in range(width // LANES)]
    return [tiles[p : p + 2] for p in range(0, len(tiles), 2)]


def spread(ref, value):
    order, part, width = value.shape
    for t in range(width // LANES):
        ref[t] = value[:, :, t * LANES : (t + 1) * LANES].astype(F32).reshape(order * part, LANES)


def take(ref, pair, order, part):
    got = [ref[t, pl.ds(j, order, stride=part), :] for j, t in pair]
    return jnp.concatenate(got, axis=1).astype(BF16)


def put(ref, pair, order, part, value):
    for n, (j, t) in enumerate(pair):
        ref[t, pl.ds(j, order, stride=part), :] = value[:, n * LANES : (n + 1) * LANES]


def gather(ref, members, part):
    tiles = [ref[t].reshape(members, -1, part, LANES).astype(BF16) for t in range(ref.shape[0])]
    return jnp.concatenate(tiles, axis=-1)


def pick(ref, pair):
    return jnp.concatenate([ref[j, :, t * LANES : (t + 1) * LANES] for j, t in pair], axis=1)


def backward_mixed(moved, kernel, outer, back, members):
    order, part, channels = moved.shape
    width = min(channels, 2 * LANES)
    local = order // members

    def body(m_ref, k_ref, o_ref, b_ref, gw_ref, gf_ref, held, result):
        spread(held, m_ref[...])
        for pair in tile_pairs(part, width):
            mixed = dot(b_ref[...], take(held, pair, order, part), (0, 0))
            gw = (mixed * pick(k_ref, pair).astype(F32)).astype(BF16)
            for n, (j, t) in enumerate(pair):
                gw_ref[j, :, t * LANES : (t + 1) * LANES] = gw[:, n * LANES : (n + 1) * LANES]
            put(result, pair, order, part, dot(o_ref[...], gw, (0, 0)))
        gf_ref[...] = gather(result, members, part)

    return call(
        body,
        (channels // width,),
        [
            pl.BlockSpec((order, part, width), lambda g: (0, 0, g)),
            pl.BlockSpec((part, order, width), lambda g: (0, 0, g)),
            square(order),
            square(order),
        ],
        [
            (
                pl.BlockSpec((part, order, width), lambda g: (0, 0, g)),
                jax.ShapeDtypeStruct((part, order, channels), BF16),
            ),
            (
                pl.BlockSpec((members, local, part, width), lambda g: (0, 0, 0, g)),
                jax.ShapeDtypeStruct((members, local, part, channels), BF16),
            ),
        ],
        [pltpu.VMEM((width // LANES, order * part, LANES), F32)] * 2,
        4 * order * moved.size,
        8 * moved.size,
    )(moved, kernel, outer, back)


def forward_mixed(first, grad_ret, kernel, gw, outer, back, members):
    order, part, channels = first.shape
    width = min(channels, 2 * LANES)
    local = order // members

    def body(f_ref, g_ref, k_ref, gw_ref, o_ref, b_ref, ret_ref, go_ref, gr_ref, held, held_g, result):
        @pl.when(pl.program_id(0) == 0)
        def _():
            go_ref[...] = jnp.zeros_like(go_ref)
            gr_ref[...] = jnp.zeros_like(gr_ref)

        spread(held, f_ref[...])
        spread(held_g, g_ref[...])
        for pair in tile_pairs(part, width):
            first_j = take(held, pair, order, part)
            mixed = dot(o_ref[...], first_j, (1, 0))
            weighted = (mixed * pick(k_ref, pair).astype(F32)).astype(BF16)
            put(result, pair, order, part, dot(b_ref[...], weighted, (1, 0)))
            go_ref[...] += dot(pick(gw_ref, pair), first_j, (1, 1))
            gr_ref[...] += dot(take(held_g, pair, order, part), weighted, (1, 1))
        ret_ref[...] = gather(result, members, part)

    moved = pl.BlockSpec((order, part, width), lambda g: (0, 0, g))
    mine = pl.BlockSpec((part, order, width), lambda g: (0, 0, g))
    small = (square(order), jax.ShapeDtypeStruct((order, order), F32))
    return call(
        body,
        (channels // width,),
        [moved, moved, mine, mine, square(order), square(order)],
        [
            (
                pl.BlockSpec((members, local, part, width), lambda g: (0, 0, 0, g)),
                jax.ShapeDtypeStruct((members, local, part, channels), BF16),
            ),
            small,
            small,
        ],
        [pltpu.VMEM((width // LANES, order * part, LANES), F32)] * 3,
        8 * order * first.size,
        10 * first.size,
    )(first, grad_ret, kernel, gw, outer, back)


def finish_values(grad_first, values, inner):
    members, rows, part, channels = grad_first.shape
    order = members * part
    step = max(1, rows // 4)

    def body(g_ref, v_ref, f_ref, gv_ref, gi_ref):
        @pl.when(pl.program_id(0) == 0)
        def _():
            gi_ref[...] = jnp.zeros_like(gi_ref)

        for r in range(step):
            g = g_ref[:, r].astype(F32).reshape(order, channels).astype(BF16)
            gv_ref[r] = dot(f_ref[...], g, (0, 0)).astype(BF16)
            gi_ref[...] += dot(g, v_ref[r], (1, 1))

    rowed = pl.BlockSpec((step, order, channels), lambda g: (g, 0, 0))
    return call(
        body,
        (rows // step,),
        [pl.BlockSpec((members, step, part, channels), lambda g: (0, g, 0, 0)), rowed, square(order)],
        [
            (rowed, jax.ShapeDtypeStruct(values.shape, BF16)),
            (square(order), jax.ShapeDtypeStruct((order, order), F32)),
        ],
        [],
        4 * order * values.size,
        6 * values.size,
    )(grad_first, values, inner)


def finish_return(returned, cotangent):
    members, rows, part, channels = returned.shape
    order = members * part
    step = max(1, rows // 4)

    def body(r_ref, c_ref, o_ref):
        @pl.when(pl.program_id(0) == 0)
        def _():
            o_ref[...] = jnp.zeros_like(o_ref)

        for r in range(step):
            ret = r_ref[:, r].astype(F32).reshape(order, channels).astype(BF16)
            o_ref[...] += dot(c_ref[r], ret, (1, 1))

    return call(
        body,
        (rows // step,),
        [
            pl.BlockSpec((members, step, part, channels), lambda g: (0, g, 0, 0)),
            pl.BlockSpec((step, order, channels), lambda g: (g, 0, 0)),
        ],
        [(square(order), jax.ShapeDtypeStruct((order, order), F32))],
        [],
        2 * order * cotangent.size,
        4 * cotangent.size,
    )(returned, cotangent)[0]


def plain(values, kernel, cotangent, inner_factor, outer_factor, return_outer, return_inner):
    f32 = F32
    bf16 = BF16
    order_a = outer_factor.shape[0]
    order_b = inner_factor.shape[0]
    channels = kernel.shape[2]
    seq_count = values.shape[0] * lax.axis_size("dp")
    scale_a = 1.0 / math.sqrt(seq_count * order_a * channels)
    scale_b = 1.0 / math.sqrt(seq_count * order_b * channels)
    first = jnp.einsum("jb,sabc->sajc", inner_factor, values, preferred_element_type=f32).astype(
        bf16
    )
    piece = lax.all_to_all(first, "seq", split_axis=2, concat_axis=1, tiled=True)
    mixed = jnp.einsum("ia,sajc->sjic", outer_factor, piece, preferred_element_type=f32)
    first_moved = piece
    weighted = (mixed * kernel[None].astype(f32)).astype(bf16)
    returned_local = jnp.einsum(
        "ki,sjic->sjkc", return_outer, weighted, preferred_element_type=f32
    ).astype(bf16)
    returned = lax.all_to_all(returned_local, "seq", split_axis=2, concat_axis=1, tiled=True)
    grad_returned = jnp.einsum(
        "lj,sklc->skjc", return_inner, cotangent, preferred_element_type=f32
    ).astype(bf16)
    grad_gtwo = jnp.einsum("sklc,sjkc->lj", cotangent, returned, preferred_element_type=f32)
    piece = lax.all_to_all(grad_returned, "seq", split_axis=2, concat_axis=1, tiled=True)
    grad_mixed = jnp.einsum("ki,skjc->sjic", return_outer, piece, preferred_element_type=f32)
    grad_ret_moved = piece
    grad_gone = jnp.einsum("skjc,sjic->ki", grad_ret_moved, weighted, preferred_element_type=f32)
    grad_weighted = (grad_mixed * kernel[None].astype(f32)).astype(bf16)
    grad_first_moved = jnp.einsum(
        "ia,sjic->sajc", outer_factor, grad_weighted, preferred_element_type=f32
    ).astype(bf16)
    grad_ftwo = jnp.einsum("sjic,sajc->ia", grad_weighted, first_moved, preferred_element_type=f32)
    piece = lax.all_to_all(grad_first_moved, "seq", split_axis=1, concat_axis=2, tiled=True)
    grad_values = jnp.einsum(
        "jb,sajc->sabc", inner_factor, piece, preferred_element_type=f32
    ).astype(bf16)
    grad_fone = jnp.einsum("sajc,sabc->jb", piece, values, preferred_element_type=f32)
    summed = lax.psum((grad_fone, grad_ftwo, grad_gone, grad_gtwo), ("seq", "dp"))
    return (
        grad_values,
        summed[0] * scale_a,
        summed[1] * scale_b,
        summed[2] * scale_b,
        summed[3] * scale_a,
    )


def swap(x, bits):
    size = lax.axis_size("seq")
    return lax.ppermute(x, "seq", [(i, i ^ bits) for i in range(size)])


def exchange(x, members):
    size = lax.axis_size("seq")
    groups = [list(range(g, g + members)) for g in range(0, size, members)]
    return lax.all_to_all(x, "seq", 0, 0, axis_index_groups=groups, tiled=True)


def total(x):
    rows, columns = x.shape
    parts = exchange(x.astype(BF16).reshape(8, rows // 8, columns), 8)
    held = jnp.sum(parts.astype(F32), axis=0)
    held = held + swap(held, 16)
    held = held + swap(held, 8)
    out = jnp.broadcast_to(held[None], (8, rows // 8, columns))
    return exchange(out, 8).reshape(rows, columns)


class Part:
    def __init__(self, low, members):
        self.low = low
        self.members = members
        self.splits = lax.axis_size("seq") // members
        self.mine = lax.axis_index("seq") // members

    def lanes(self, split):
        return self.low + split * LANES

    def bring(self, x):
        rows, order, _ = x.shape
        out = jnp.zeros((self.splits * rows, order, LANES), BF16)
        for d in range(self.splits):
            other = self.mine ^ d
            piece = lax.dynamic_slice(x, (0, 0, self.lanes(other)), (rows, order, LANES))
            piece = swap(piece, d * self.members) if d else piece
            out = lax.dynamic_update_slice(out, piece, (other * rows, 0, 0))
        return out

    def give(self, out, x):
        rows, order, _ = out.shape
        for d in range(self.splits):
            other = self.mine ^ d
            piece = lax.dynamic_slice(x, (other * rows, 0, 0), (rows, order, LANES))
            piece = swap(piece, d * self.members) if d else piece
            out = lax.dynamic_update_slice(out, piece, (0, 0, self.lanes(other)))
        return out

    def sort(self, matrix, axis, back=False):
        shape = matrix.shape
        s, m = self.splits, self.members
        cut = (m, s) if back else (s, m)
        cut = shape[:axis] + cut + (shape[axis] // (s * m),) + shape[axis + 1 :]
        return jnp.swapaxes(matrix.reshape(cut), axis, axis + 1).reshape(shape)


def per_device(values, kernel, cotangent, inner_factor, outer_factor, return_outer, return_inner):
    size = lax.axis_size("seq")
    order = outer_factor.shape[0]
    rows, channels = kernel.shape[0], kernel.shape[2]
    if (
        size != 32
        or lax.axis_size("dp") != 1
        or values.shape[0] != 1
        or rows != 8
        or inner_factor.shape[0] != order
        or channels != 6 * LANES
    ):
        return plain(
            values, kernel, cotangent, inner_factor, outer_factor, return_outer, return_inner
        )
    scale = 1.0 / math.sqrt(order * channels)
    grads = []
    out = jnp.zeros(values.shape[1:], BF16)
    for part in (Part(0, 8), Part(4 * LANES, 16)):
        m = part.members
        inner = part.sort(inner_factor, 0)
        outer = part.sort(outer_factor, 1)
        back = part.sort(return_outer, 0)
        last = part.sort(return_inner, 1)

        cot = part.bring(cotangent[0])
        ker = part.bring(kernel)
        val = part.bring(values[0])
        flat = (order, cot.shape[0], LANES)
        grad_ret = exchange(apply_inner(cot, last, 0, m), m).reshape(flat)
        gw, sent = backward_mixed(grad_ret, ker, outer, back, m)
        grad_first = exchange(sent, m)
        first = exchange(apply_inner(val, inner, 1, m), m).reshape(flat)
        sent, grad_outer, grad_back = forward_mixed(first, grad_ret, ker, gw, outer, back, m)
        returned = exchange(sent, m)
        grad_values, grad_inner = finish_values(grad_first, val, inner)
        grad_last = finish_return(returned, cot)
        out = part.give(out, grad_values)
        grads.append(
            (
                part.sort(grad_inner, 0, True),
                part.sort(grad_outer, 1, True),
                part.sort(grad_back, 0, True),
                part.sort(grad_last, 1, True),
            )
        )
    grads = total(jnp.concatenate([sum(g) for g in zip(*grads)], axis=1)) * scale
    return (out[None], *jnp.split(grads, 4, axis=1))


def solution(mesh):
    return jax.shard_map(
        per_device,
        mesh=mesh,
        in_specs=(
            P(("groups", "dp"), "seq", None, None),
            P("seq", None, None),
            P(("groups", "dp"), "seq", None, None),
            P(),
            P(),
            P(),
            P(),
        ),
        out_specs=(
            P(("groups", "dp"), "seq", None, None),
            P("groups", None),
            P("groups", None),
            P("groups", None),
            P("groups", None),
        ),
        check_vma=False,
    )
```

```python
import math

import jax
import jax.numpy as jnp
from jax import lax
from jax.experimental import pallas as pl
from jax.experimental.pallas import tpu as pltpu
from jax.sharding import PartitionSpec as P

F32 = jnp.float32
BF16 = jnp.bfloat16
LANES = 128
VMEM = 63 * 2**20


def dot(x, y, dims):
    return lax.dot_general(x, y, ((dims[:1], dims[1:]), ((), ())), preferred_element_type=F32)


def call(body, grid, ins, outs, scratch, flops, moved):
    return pl.pallas_call(
        body,
        grid=grid,
        in_specs=[spec for spec in ins],
        out_specs=[spec for spec, _ in outs],
        out_shape=[shape for _, shape in outs],
        scratch_shapes=scratch,
        compiler_params=pltpu.CompilerParams(
            vmem_limit_bytes=VMEM, dimension_semantics=("arbitrary",) * len(grid)
        ),
        cost_estimate=pl.CostEstimate(flops=flops, bytes_accessed=moved, transcendentals=0),
    )


def square(order):
    return pl.BlockSpec((order, order), lambda *g: (0, 0))


def apply_inner(x, factor, side, members):
    rows, order, channels = x.shape
    part = order // members
    step = max(1, rows // 2)

    def body(x_ref, f_ref, o_ref):
        for r in range(step):
            y = dot(f_ref[...], x_ref[r], (side, 0))
            o_ref[:, r] = y.reshape(members, part, channels).astype(BF16)

    return call(
        body,
        (rows // step,),
        [pl.BlockSpec((step, order, channels), lambda g: (g, 0, 0)), square(order)],
        [
            (
                pl.BlockSpec((members, step, part, channels), lambda g: (0, g, 0, 0)),
                jax.ShapeDtypeStruct((members, rows, part, channels), BF16),
            )
        ],
        [],
        2 * order * x.size,
        4 * x.size,
    )(x, factor)[0]


def tile_pairs(part, width):
    tiles = [(j, t) for j in range(part) for t in range(width // LANES)]
    return [tiles[p : p + 2] for p in range(0, len(tiles), 2)]


def spread(ref, value):
    order, part, width = value.shape
    for t in range(width // LANES):
        ref[t] = value[:, :, t * LANES : (t + 1) * LANES].astype(F32).reshape(order * part, LANES)


def take(ref, pair, order, part):
    got = [ref[t, pl.ds(j, order, stride=part), :] for j, t in pair]
    return jnp.concatenate(got, axis=1).astype(BF16)


def put(ref, pair, order, part, value):
    for n, (j, t) in enumerate(pair):
        ref[t, pl.ds(j, order, stride=part), :] = value[:, n * LANES : (n + 1) * LANES]


def gather(ref, members, part):
    tiles = [ref[t].reshape(members, -1, part, LANES).astype(BF16) for t in range(ref.shape[0])]
    return jnp.concatenate(tiles, axis=-1)


def pick(ref, pair):
    return jnp.concatenate([ref[j, :, t * LANES : (t + 1) * LANES] for j, t in pair], axis=1)


def backward_mixed(moved, kernel, outer, back, members):
    order, part, channels = moved.shape
    width = min(channels, 2 * LANES)
    local = order // members

    def body(m_ref, k_ref, o_ref, b_ref, gw_ref, gf_ref, held, result):
        spread(held, m_ref[...])
        for pair in tile_pairs(part, width):
            mixed = dot(b_ref[...], take(held, pair, order, part), (0, 0))
            gw = (mixed * pick(k_ref, pair).astype(F32)).astype(BF16)
            for n, (j, t) in enumerate(pair):
                gw_ref[j, :, t * LANES : (t + 1) * LANES] = gw[:, n * LANES : (n + 1) * LANES]
            put(result, pair, order, part, dot(o_ref[...], gw, (0, 0)))
        gf_ref[...] = gather(result, members, part)

    return call(
        body,
        (channels // width,),
        [
            pl.BlockSpec((order, part, width), lambda g: (0, 0, g)),
            pl.BlockSpec((part, order, width), lambda g: (0, 0, g)),
            square(order),
            square(order),
        ],
        [
            (
                pl.BlockSpec((part, order, width), lambda g: (0, 0, g)),
                jax.ShapeDtypeStruct((part, order, channels), BF16),
            ),
            (
                pl.BlockSpec((members, local, part, width), lambda g: (0, 0, 0, g)),
                jax.ShapeDtypeStruct((members, local, part, channels), BF16),
            ),
        ],
        [pltpu.VMEM((width // LANES, order * part, LANES), F32)] * 2,
        4 * order * moved.size,
        8 * moved.size,
    )(moved, kernel, outer, back)


def forward_mixed(first, grad_ret, kernel, gw, outer, back, members):
    order, part, channels = first.shape
    width = min(channels, 2 * LANES)
    local = order // members

    def body(f_ref, g_ref, k_ref, gw_ref, o_ref, b_ref, ret_ref, go_ref, gr_ref, held, held_g, result):
        @pl.when(pl.program_id(0) == 0)
        def _():
            go_ref[...] = jnp.zeros_like(go_ref)
            gr_ref[...] = jnp.zeros_like(gr_ref)

        spread(held, f_ref[...])
        spread(held_g, g_ref[...])
        for pair in tile_pairs(part, width):
            first_j = take(held, pair, order, part)
            mixed = dot(o_ref[...], first_j, (1, 0))
            weighted = (mixed * pick(k_ref, pair).astype(F32)).astype(BF16)
            put(result, pair, order, part, dot(b_ref[...], weighted, (1, 0)))
            go_ref[...] += dot(pick(gw_ref, pair), first_j, (1, 1))
            gr_ref[...] += dot(take(held_g, pair, order, part), weighted, (1, 1))
        ret_ref[...] = gather(result, members, part)

    moved = pl.BlockSpec((order, part, width), lambda g: (0, 0, g))
    mine = pl.BlockSpec((part, order, width), lambda g: (0, 0, g))
    small = (square(order), jax.ShapeDtypeStruct((order, order), F32))
    return call(
        body,
        (channels // width,),
        [moved, moved, mine, mine, square(order), square(order)],
        [
            (
                pl.BlockSpec((members, local, part, width), lambda g: (0, 0, 0, g)),
                jax.ShapeDtypeStruct((members, local, part, channels), BF16),
            ),
            small,
            small,
        ],
        [pltpu.VMEM((width // LANES, order * part, LANES), F32)] * 3,
        8 * order * first.size,
        10 * first.size,
    )(first, grad_ret, kernel, gw, outer, back)


def finish_values(grad_first, values, inner):
    members, rows, part, channels = grad_first.shape
    order = members * part
    step = max(1, rows // 2)

    def body(g_ref, v_ref, f_ref, gv_ref, gi_ref):
        @pl.when(pl.program_id(0) == 0)
        def _():
            gi_ref[...] = jnp.zeros_like(gi_ref)

        for r in range(step):
            g = g_ref[:, r].astype(F32).reshape(order, channels).astype(BF16)
            gv_ref[r] = dot(f_ref[...], g, (0, 0)).astype(BF16)
            gi_ref[...] += dot(g, v_ref[r], (1, 1))

    rowed = pl.BlockSpec((step, order, channels), lambda g: (g, 0, 0))
    return call(
        body,
        (rows // step,),
        [pl.BlockSpec((members, step, part, channels), lambda g: (0, g, 0, 0)), rowed, square(order)],
        [
            (rowed, jax.ShapeDtypeStruct(values.shape, BF16)),
            (square(order), jax.ShapeDtypeStruct((order, order), F32)),
        ],
        [],
        4 * order * values.size,
        6 * values.size,
    )(grad_first, values, inner)


def finish_return(returned, cotangent):
    members, rows, part, channels = returned.shape
    order = members * part
    step = max(1, rows // 2)

    def body(r_ref, c_ref, o_ref):
        @pl.when(pl.program_id(0) == 0)
        def _():
            o_ref[...] = jnp.zeros_like(o_ref)

        for r in range(step):
            ret = r_ref[:, r].astype(F32).reshape(order, channels).astype(BF16)
            o_ref[...] += dot(c_ref[r], ret, (1, 1))

    return call(
        body,
        (rows // step,),
        [
            pl.BlockSpec((members, step, part, channels), lambda g: (0, g, 0, 0)),
            pl.BlockSpec((step, order, channels), lambda g: (g, 0, 0)),
        ],
        [(square(order), jax.ShapeDtypeStruct((order, order), F32))],
        [],
        2 * order * cotangent.size,
        4 * cotangent.size,
    )(returned, cotangent)[0]


def plain(values, kernel, cotangent, inner_factor, outer_factor, return_outer, return_inner):
    f32 = F32
    bf16 = BF16
    order_a = outer_factor.shape[0]
    order_b = inner_factor.shape[0]
    channels = kernel.shape[2]
    seq_count = values.shape[0] * lax.axis_size("dp")
    scale_a = 1.0 / math.sqrt(seq_count * order_a * channels)
    scale_b = 1.0 / math.sqrt(seq_count * order_b * channels)
    first = jnp.einsum("jb,sabc->sajc", inner_factor, values, preferred_element_type=f32).astype(
        bf16
    )
    piece = lax.all_to_all(first, "seq", split_axis=2, concat_axis=1, tiled=True)
    mixed = jnp.einsum("ia,sajc->sjic", outer_factor, piece, preferred_element_type=f32)
    first_moved = piece
    weighted = (mixed * kernel[None].astype(f32)).astype(bf16)
    returned_local = jnp.einsum(
        "ki,sjic->sjkc", return_outer, weighted, preferred_element_type=f32
    ).astype(bf16)
    returned = lax.all_to_all(returned_local, "seq", split_axis=2, concat_axis=1, tiled=True)
    grad_returned = jnp.einsum(
        "lj,sklc->skjc", return_inner, cotangent, preferred_element_type=f32
    ).astype(bf16)
    grad_gtwo = jnp.einsum("sklc,sjkc->lj", cotangent, returned, preferred_element_type=f32)
    piece = lax.all_to_all(grad_returned, "seq", split_axis=2, concat_axis=1, tiled=True)
    grad_mixed = jnp.einsum("ki,skjc->sjic", return_outer, piece, preferred_element_type=f32)
    grad_ret_moved = piece
    grad_gone = jnp.einsum("skjc,sjic->ki", grad_ret_moved, weighted, preferred_element_type=f32)
    grad_weighted = (grad_mixed * kernel[None].astype(f32)).astype(bf16)
    grad_first_moved = jnp.einsum(
        "ia,sjic->sajc", outer_factor, grad_weighted, preferred_element_type=f32
    ).astype(bf16)
    grad_ftwo = jnp.einsum("sjic,sajc->ia", grad_weighted, first_moved, preferred_element_type=f32)
    piece = lax.all_to_all(grad_first_moved, "seq", split_axis=1, concat_axis=2, tiled=True)
    grad_values = jnp.einsum(
        "jb,sajc->sabc", inner_factor, piece, preferred_element_type=f32
    ).astype(bf16)
    grad_fone = jnp.einsum("sajc,sabc->jb", piece, values, preferred_element_type=f32)
    summed = lax.psum((grad_fone, grad_ftwo, grad_gone, grad_gtwo), ("seq", "dp"))
    return (
        grad_values,
        summed[0] * scale_a,
        summed[1] * scale_b,
        summed[2] * scale_b,
        summed[3] * scale_a,
    )


def swap(x, bits):
    size = lax.axis_size("seq")
    return lax.ppermute(x, "seq", [(i, i ^ bits) for i in range(size)])


def move(x):
    return lax.all_to_all(x, "seq", 0, 0, tiled=True)


def halves(x, bit):
    mine = (lax.axis_index("seq") // bit) % 2
    pair = x.reshape(2, x.shape[0] // 2, x.shape[1])
    return (
        lax.dynamic_index_in_dim(pair, mine, 0, keepdims=False),
        lax.dynamic_index_in_dim(pair, 1 - mine, 0, keepdims=False),
    )


def join(mine, other, bit):
    first = (lax.axis_index("seq") // bit) % 2 == 0
    return jnp.concatenate((jnp.where(first, mine, other), jnp.where(first, other, mine)), axis=0)


def early_sum(x):
    for bit in (1, 2, 4):
        keep, give = halves(x, bit)
        x = keep + swap(give, bit)
    for bit in (16, 8):
        x = x.astype(BF16)
        x = x.astype(F32) + swap(x, bit).astype(F32)
    for bit in (4, 2, 1):
        x = join(x, swap(x, bit), bit)
    return x


def late_sum(x):
    size = lax.axis_size("seq")
    rows, columns = x.shape
    parts = move(x.astype(BF16).reshape(size, rows // size, columns))
    held = jnp.sum(parts.astype(F32), axis=0)
    return move(jnp.broadcast_to(held[None], parts.shape)).reshape(rows, columns)


def per_device(values, kernel, cotangent, inner_factor, outer_factor, return_outer, return_inner):
    members = lax.axis_size("seq")
    order = outer_factor.shape[0]
    rows, channels = kernel.shape[0], kernel.shape[2]
    if (
        members != 32
        or lax.axis_size("dp") != 1
        or values.shape[0] != 1
        or rows != 8
        or inner_factor.shape[0] != order
        or channels % (2 * LANES)
    ):
        return plain(
            values, kernel, cotangent, inner_factor, outer_factor, return_outer, return_inner
        )
    scale = 1.0 / math.sqrt(order * channels)

    grad_ret = move(apply_inner(cotangent[0], return_inner, 0, members))
    sent = apply_inner(values[0], inner_factor, 1, members)
    sent, grad_ret = lax.optimization_barrier((sent, grad_ret))
    first = move(sent)
    grad_ret = grad_ret.reshape(order, rows, channels)
    gw, sent = backward_mixed(grad_ret, kernel, outer_factor, return_outer, members)
    sent, first = lax.optimization_barrier((sent, first))
    grad_first = move(sent)
    first = first.reshape(order, rows, channels)
    sent, grad_outer, grad_back = forward_mixed(
        first, grad_ret, kernel, gw, outer_factor, return_outer, members
    )
    sent, grad_first = lax.optimization_barrier((sent, grad_first))
    returned = move(sent)
    grad_values, grad_inner = finish_values(grad_first, values[0], inner_factor)
    early = early_sum(jnp.concatenate((grad_inner, grad_outer, grad_back), axis=1)) * scale
    returned, early = lax.optimization_barrier((returned, early))
    grad_last = late_sum(finish_return(returned, cotangent[0])) * scale
    return (grad_values[None], *jnp.split(early, 3, axis=1), grad_last)


def solution(mesh):
    return jax.shard_map(
        per_device,
        mesh=mesh,
        in_specs=(
            P(("groups", "dp"), "seq", None, None),
            P("seq", None, None),
            P(("groups", "dp"), "seq", None, None),
            P(),
            P(),
            P(),
            P(),
        ),
        out_specs=(
            P(("groups", "dp"), "seq", None, None),
            P("groups", None),
            P("groups", None),
            P("groups", None),
            P("groups", None),
        ),
        check_vma=False,
    )
```

```python
import math

import jax
import jax.numpy as jnp
from jax import lax
from jax.experimental import pallas as pl
from jax.experimental.pallas import tpu as pltpu
from jax.sharding import PartitionSpec as P

F32 = jnp.float32
BF16 = jnp.bfloat16
LANES = 128
VMEM = 63 * 2**20


def dot(x, y, dims):
    return lax.dot_general(x, y, ((dims[:1], dims[1:]), ((), ())), preferred_element_type=F32)


def call(body, grid, ins, outs, scratch, flops, moved):
    return pl.pallas_call(
        body,
        grid=grid,
        in_specs=[spec for spec in ins],
        out_specs=[spec for spec, _ in outs],
        out_shape=[shape for _, shape in outs],
        scratch_shapes=scratch,
        compiler_params=pltpu.CompilerParams(
            vmem_limit_bytes=VMEM, dimension_semantics=("arbitrary",) * len(grid)
        ),
        cost_estimate=pl.CostEstimate(flops=flops, bytes_accessed=moved, transcendentals=0),
    )


def square(order):
    return pl.BlockSpec((order, order), lambda *g: (0, 0))


def apply_inner(x, factor, side, members):
    rows, order, channels = x.shape
    part = order // members
    step = max(1, rows // 2)

    def body(x_ref, f_ref, o_ref):
        for r in range(step):
            y = dot(f_ref[...], x_ref[r], (side, 0))
            o_ref[:, r] = y.reshape(members, part, channels).astype(BF16)

    return call(
        body,
        (rows // step,),
        [pl.BlockSpec((step, order, channels), lambda g: (g, 0, 0)), square(order)],
        [
            (
                pl.BlockSpec((members, step, part, channels), lambda g: (0, g, 0, 0)),
                jax.ShapeDtypeStruct((members, rows, part, channels), BF16),
            )
        ],
        [],
        2 * order * x.size,
        4 * x.size,
    )(x, factor)[0]


def tile_pairs(part, width):
    tiles = [(j, t) for j in range(part) for t in range(width // LANES)]
    return [tiles[p : p + 2] for p in range(0, len(tiles), 2)]


def spread(ref, value):
    order, part, width = value.shape
    for t in range(width // LANES):
        ref[t] = value[:, :, t * LANES : (t + 1) * LANES].astype(F32).reshape(order * part, LANES)


def take(ref, pair, order, part):
    got = [ref[t, pl.ds(j, order, stride=part), :] for j, t in pair]
    return jnp.concatenate(got, axis=1).astype(BF16)


def put(ref, pair, order, part, value):
    for n, (j, t) in enumerate(pair):
        ref[t, pl.ds(j, order, stride=part), :] = value[:, n * LANES : (n + 1) * LANES]


def gather(ref, members, part):
    tiles = [ref[t].reshape(members, -1, part, LANES).astype(BF16) for t in range(ref.shape[0])]
    return jnp.concatenate(tiles, axis=-1)


def pick(ref, pair):
    return jnp.concatenate([ref[j, :, t * LANES : (t + 1) * LANES] for j, t in pair], axis=1)


def backward_mixed(moved, kernel, outer, back, members):
    order, part, channels = moved.shape
    width = min(channels, 2 * LANES)
    local = order // members

    def body(m_ref, k_ref, o_ref, b_ref, gw_ref, gf_ref, held, result):
        spread(held, m_ref[...])
        for pair in tile_pairs(part, width):
            mixed = dot(b_ref[...], take(held, pair, order, part), (0, 0))
            gw = (mixed * pick(k_ref, pair).astype(F32)).astype(BF16)
            for n, (j, t) in enumerate(pair):
                gw_ref[j, :, t * LANES : (t + 1) * LANES] = gw[:, n * LANES : (n + 1) * LANES]
            put(result, pair, order, part, dot(o_ref[...], gw, (0, 0)))
        gf_ref[...] = gather(result, members, part)

    return call(
        body,
        (channels // width,),
        [
            pl.BlockSpec((order, part, width), lambda g: (0, 0, g)),
            pl.BlockSpec((part, order, width), lambda g: (0, 0, g)),
            square(order),
            square(order),
        ],
        [
            (
                pl.BlockSpec((part, order, width), lambda g: (0, 0, g)),
                jax.ShapeDtypeStruct((part, order, channels), BF16),
            ),
            (
                pl.BlockSpec((members, local, part, width), lambda g: (0, 0, 0, g)),
                jax.ShapeDtypeStruct((members, local, part, channels), BF16),
            ),
        ],
        [pltpu.VMEM((width // LANES, order * part, LANES), F32)] * 2,
        4 * order * moved.size,
        8 * moved.size,
    )(moved, kernel, outer, back)


def forward_mixed(first, grad_ret, kernel, gw, outer, back, members):
    order, part, channels = first.shape
    width = min(channels, 2 * LANES)
    local = order // members

    def body(f_ref, g_ref, k_ref, gw_ref, o_ref, b_ref, ret_ref, go_ref, gr_ref, held, held_g, result):
        @pl.when(pl.program_id(0) == 0)
        def _():
            go_ref[...] = jnp.zeros_like(go_ref)
            gr_ref[...] = jnp.zeros_like(gr_ref)

        spread(held, f_ref[...])
        spread(held_g, g_ref[...])
        for pair in tile_pairs(part, width):
            first_j = take(held, pair, order, part)
            mixed = dot(o_ref[...], first_j, (1, 0))
            weighted = (mixed * pick(k_ref, pair).astype(F32)).astype(BF16)
            put(result, pair, order, part, dot(b_ref[...], weighted, (1, 0)))
            go_ref[...] += dot(pick(gw_ref, pair), first_j, (1, 1))
            gr_ref[...] += dot(take(held_g, pair, order, part), weighted, (1, 1))
        ret_ref[...] = gather(result, members, part)

    moved = pl.BlockSpec((order, part, width), lambda g: (0, 0, g))
    mine = pl.BlockSpec((part, order, width), lambda g: (0, 0, g))
    small = (square(order), jax.ShapeDtypeStruct((order, order), F32))
    return call(
        body,
        (channels // width,),
        [moved, moved, mine, mine, square(order), square(order)],
        [
            (
                pl.BlockSpec((members, local, part, width), lambda g: (0, 0, 0, g)),
                jax.ShapeDtypeStruct((members, local, part, channels), BF16),
            ),
            small,
            small,
        ],
        [pltpu.VMEM((width // LANES, order * part, LANES), F32)] * 3,
        8 * order * first.size,
        10 * first.size,
    )(first, grad_ret, kernel, gw, outer, back)


def finish_values(grad_first, values, inner):
    members, rows, part, channels = grad_first.shape
    order = members * part
    step = max(1, rows // 2)

    def body(g_ref, v_ref, f_ref, gv_ref, gi_ref):
        @pl.when(pl.program_id(0) == 0)
        def _():
            gi_ref[...] = jnp.zeros_like(gi_ref)

        for r in range(step):
            g = g_ref[:, r].astype(F32).reshape(order, channels).astype(BF16)
            gv_ref[r] = dot(f_ref[...], g, (0, 0)).astype(BF16)
            gi_ref[...] += dot(g, v_ref[r], (1, 1))

    rowed = pl.BlockSpec((step, order, channels), lambda g: (g, 0, 0))
    return call(
        body,
        (rows // step,),
        [pl.BlockSpec((members, step, part, channels), lambda g: (0, g, 0, 0)), rowed, square(order)],
        [
            (rowed, jax.ShapeDtypeStruct(values.shape, BF16)),
            (square(order), jax.ShapeDtypeStruct((order, order), F32)),
        ],
        [],
        4 * order * values.size,
        6 * values.size,
    )(grad_first, values, inner)


def finish_return(returned, cotangent):
    members, rows, part, channels = returned.shape
    order = members * part
    step = max(1, rows // 2)
    steps = rows // step

    def body(r_ref, c_ref, o_ref, acc):
        @pl.when(pl.program_id(0) == 0)
        def _():
            acc[...] = jnp.zeros_like(acc)

        for r in range(step):
            ret = r_ref[:, r].astype(F32).reshape(order, channels).astype(BF16)
            acc[...] += dot(c_ref[r], ret, (1, 1))

        @pl.when(pl.program_id(0) == steps - 1)
        def _():
            o_ref[...] = acc[...].astype(BF16)

    return call(
        body,
        (steps,),
        [
            pl.BlockSpec((members, step, part, channels), lambda g: (0, g, 0, 0)),
            pl.BlockSpec((step, order, channels), lambda g: (g, 0, 0)),
        ],
        [(square(order), jax.ShapeDtypeStruct((order, order), BF16))],
        [pltpu.VMEM((order, order), F32)],
        2 * order * cotangent.size,
        4 * cotangent.size,
    )(returned, cotangent)[0]


def plain(values, kernel, cotangent, inner_factor, outer_factor, return_outer, return_inner):
    f32 = F32
    bf16 = BF16
    order_a = outer_factor.shape[0]
    order_b = inner_factor.shape[0]
    channels = kernel.shape[2]
    seq_count = values.shape[0] * lax.axis_size("dp")
    scale_a = 1.0 / math.sqrt(seq_count * order_a * channels)
    scale_b = 1.0 / math.sqrt(seq_count * order_b * channels)
    first = jnp.einsum("jb,sabc->sajc", inner_factor, values, preferred_element_type=f32).astype(
        bf16
    )
    piece = lax.all_to_all(first, "seq", split_axis=2, concat_axis=1, tiled=True)
    mixed = jnp.einsum("ia,sajc->sjic", outer_factor, piece, preferred_element_type=f32)
    first_moved = piece
    weighted = (mixed * kernel[None].astype(f32)).astype(bf16)
    returned_local = jnp.einsum(
        "ki,sjic->sjkc", return_outer, weighted, preferred_element_type=f32
    ).astype(bf16)
    returned = lax.all_to_all(returned_local, "seq", split_axis=2, concat_axis=1, tiled=True)
    grad_returned = jnp.einsum(
        "lj,sklc->skjc", return_inner, cotangent, preferred_element_type=f32
    ).astype(bf16)
    grad_gtwo = jnp.einsum("sklc,sjkc->lj", cotangent, returned, preferred_element_type=f32)
    piece = lax.all_to_all(grad_returned, "seq", split_axis=2, concat_axis=1, tiled=True)
    grad_mixed = jnp.einsum("ki,skjc->sjic", return_outer, piece, preferred_element_type=f32)
    grad_ret_moved = piece
    grad_gone = jnp.einsum("skjc,sjic->ki", grad_ret_moved, weighted, preferred_element_type=f32)
    grad_weighted = (grad_mixed * kernel[None].astype(f32)).astype(bf16)
    grad_first_moved = jnp.einsum(
        "ia,sjic->sajc", outer_factor, grad_weighted, preferred_element_type=f32
    ).astype(bf16)
    grad_ftwo = jnp.einsum("sjic,sajc->ia", grad_weighted, first_moved, preferred_element_type=f32)
    piece = lax.all_to_all(grad_first_moved, "seq", split_axis=1, concat_axis=2, tiled=True)
    grad_values = jnp.einsum(
        "jb,sajc->sabc", inner_factor, piece, preferred_element_type=f32
    ).astype(bf16)
    grad_fone = jnp.einsum("sajc,sabc->jb", piece, values, preferred_element_type=f32)
    summed = lax.psum((grad_fone, grad_ftwo, grad_gone, grad_gtwo), ("seq", "dp"))
    return (
        grad_values,
        summed[0] * scale_a,
        summed[1] * scale_b,
        summed[2] * scale_b,
        summed[3] * scale_a,
    )


def swap(x, bits):
    size = lax.axis_size("seq")
    return lax.ppermute(x, "seq", [(i, i ^ bits) for i in range(size)])


def move(x):
    return lax.all_to_all(x, "seq", 0, 0, tiled=True)


def halves(x, bit):
    mine = (lax.axis_index("seq") // bit) % 2
    pair = x.reshape(2, x.shape[0] // 2, x.shape[1])
    return (
        lax.dynamic_index_in_dim(pair, mine, 0, keepdims=False),
        lax.dynamic_index_in_dim(pair, 1 - mine, 0, keepdims=False),
    )


def join(mine, other, bit):
    first = (lax.axis_index("seq") // bit) % 2 == 0
    return jnp.concatenate((jnp.where(first, mine, other), jnp.where(first, other, mine)), axis=0)


def plane_sum(x):
    for bit in (1, 2, 4):
        keep, give = halves(x, bit)
        x = keep + swap(give, bit)
    return x


def across(x):
    x = x.astype(BF16)
    near, *far = [swap(x, bits) for bits in (8, 16, 24)]
    return x, near, *far


def joined(x):
    for bit in (4, 2, 1):
        x = join(x, swap(x, bit), bit)
    return x


def late_sum(x):
    size = lax.axis_size("seq")
    rows, columns = x.shape
    parts = move(x.reshape(size, rows // size, columns))
    held = jnp.sum(parts.astype(F32), axis=0).astype(BF16)
    return move(jnp.broadcast_to(held[None], parts.shape)).reshape(rows, columns).astype(F32)


def per_device(values, kernel, cotangent, inner_factor, outer_factor, return_outer, return_inner):
    members = lax.axis_size("seq")
    order = outer_factor.shape[0]
    rows, channels = kernel.shape[0], kernel.shape[2]
    if (
        members != 32
        or lax.axis_size("dp") != 1
        or values.shape[0] != 1
        or rows != 8
        or inner_factor.shape[0] != order
        or channels % (2 * LANES)
    ):
        return plain(
            values, kernel, cotangent, inner_factor, outer_factor, return_outer, return_inner
        )
    scale = 1.0 / math.sqrt(order * channels)

    grad_ret = move(apply_inner(cotangent[0], return_inner, 0, members))
    sent = apply_inner(values[0], inner_factor, 1, members)
    sent, grad_ret = lax.optimization_barrier((sent, grad_ret))
    first = move(sent)
    grad_ret = grad_ret.reshape(order, rows, channels)
    gw, sent = backward_mixed(grad_ret, kernel, outer_factor, return_outer, members)
    sent, first = lax.optimization_barrier((sent, first))
    grad_first = move(sent)
    first = first.reshape(order, rows, channels)
    sent, grad_outer, grad_back = forward_mixed(
        first, grad_ret, kernel, gw, outer_factor, return_outer, members
    )
    sent, grad_first = lax.optimization_barrier((sent, grad_first))
    returned = move(sent)
    grad_values, grad_inner = finish_values(grad_first, values[0], inner_factor)
    early = plane_sum(jnp.concatenate((grad_inner, grad_outer, grad_back), axis=1))
    returned, early = lax.optimization_barrier((returned, early))
    quarters = across(early)
    grad_last = finish_return(returned, cotangent[0])
    (a, b, c, d), grad_last = lax.optimization_barrier((quarters, grad_last))
    early = (a.astype(F32) + b.astype(F32)) + (c.astype(F32) + d.astype(F32))
    early = joined(early) * scale
    grad_last = late_sum(grad_last) * scale
    return (grad_values[None], *jnp.split(early, 3, axis=1), grad_last)


def solution(mesh):
    return jax.shard_map(
        per_device,
        mesh=mesh,
        in_specs=(
            P(("groups", "dp"), "seq", None, None),
            P("seq", None, None),
            P(("groups", "dp"), "seq", None, None),
            P(),
            P(),
            P(),
            P(),
        ),
        out_specs=(
            P(("groups", "dp"), "seq", None, None),
            P("groups", None),
            P("groups", None),
            P("groups", None),
            P("groups", None),
        ),
        check_vma=False,
    )
```

```python
import math

import jax
import jax.numpy as jnp
from jax import lax
from jax.experimental import pallas as pl
from jax.experimental.pallas import tpu as pltpu
from jax.sharding import PartitionSpec as P

F32 = jnp.float32
BF16 = jnp.bfloat16
LANES = 128
VMEM = 63 * 2**20


def dot(x, y, dims):
    return lax.dot_general(x, y, ((dims[:1], dims[1:]), ((), ())), preferred_element_type=F32)


def call(body, grid, ins, outs, scratch, flops, moved):
    return pl.pallas_call(
        body,
        grid=grid,
        in_specs=[spec for spec in ins],
        out_specs=[spec for spec, _ in outs],
        out_shape=[shape for _, shape in outs],
        scratch_shapes=scratch,
        compiler_params=pltpu.CompilerParams(
            vmem_limit_bytes=VMEM, dimension_semantics=("arbitrary",) * len(grid)
        ),
        cost_estimate=pl.CostEstimate(flops=flops, bytes_accessed=moved, transcendentals=0),
    )


def square(order):
    return pl.BlockSpec((order, order), lambda *g: (0, 0))


def apply_inner(x, factor, side, members):
    rows, order, channels = x.shape
    part = order // members
    step = max(1, rows // 2)

    def body(x_ref, f_ref, o_ref):
        for r in range(step):
            y = dot(f_ref[...], x_ref[r], (side, 0))
            o_ref[:, r] = y.reshape(members, part, channels).astype(BF16)

    return call(
        body,
        (rows // step,),
        [pl.BlockSpec((step, order, channels), lambda g: (g, 0, 0)), square(order)],
        [
            (
                pl.BlockSpec((members, step, part, channels), lambda g: (0, g, 0, 0)),
                jax.ShapeDtypeStruct((members, rows, part, channels), BF16),
            )
        ],
        [],
        2 * order * x.size,
        4 * x.size,
    )(x, factor)[0]


def tile_pairs(part, width):
    tiles = [(j, t) for j in range(part) for t in range(width // LANES)]
    return [tiles[p : p + 2] for p in range(0, len(tiles), 2)]


def spread(ref, value):
    order, part, width = value.shape
    for t in range(width // LANES):
        ref[t] = value[:, :, t * LANES : (t + 1) * LANES].astype(F32).reshape(order * part, LANES)


def take(ref, pair, order, part):
    got = [ref[t, pl.ds(j, order, stride=part), :] for j, t in pair]
    return jnp.concatenate(got, axis=1).astype(BF16)


def put(ref, pair, order, part, value):
    for n, (j, t) in enumerate(pair):
        ref[t, pl.ds(j, order, stride=part), :] = value[:, n * LANES : (n + 1) * LANES]


def gather(ref, members, part):
    tiles = [ref[t].reshape(members, -1, part, LANES).astype(BF16) for t in range(ref.shape[0])]
    return jnp.concatenate(tiles, axis=-1)


def pick(ref, pair):
    return jnp.concatenate([ref[j, :, t * LANES : (t + 1) * LANES] for j, t in pair], axis=1)


def backward_mixed(moved, kernel, outer, back, members):
    order, part, channels = moved.shape
    width = min(channels, 2 * LANES)
    local = order // members

    def body(m_ref, k_ref, o_ref, b_ref, gw_ref, gf_ref, held, result):
        spread(held, m_ref[...])
        for pair in tile_pairs(part, width):
            mixed = dot(b_ref[...], take(held, pair, order, part), (0, 0))
            gw = (mixed * pick(k_ref, pair).astype(F32)).astype(BF16)
            for n, (j, t) in enumerate(pair):
                gw_ref[j, :, t * LANES : (t + 1) * LANES] = gw[:, n * LANES : (n + 1) * LANES]
            put(result, pair, order, part, dot(o_ref[...], gw, (0, 0)))
        gf_ref[...] = gather(result, members, part)

    return call(
        body,
        (channels // width,),
        [
            pl.BlockSpec((order, part, width), lambda g: (0, 0, g)),
            pl.BlockSpec((part, order, width), lambda g: (0, 0, g)),
            square(order),
            square(order),
        ],
        [
            (
                pl.BlockSpec((part, order, width), lambda g: (0, 0, g)),
                jax.ShapeDtypeStruct((part, order, channels), BF16),
            ),
            (
                pl.BlockSpec((members, local, part, width), lambda g: (0, 0, 0, g)),
                jax.ShapeDtypeStruct((members, local, part, channels), BF16),
            ),
        ],
        [pltpu.VMEM((width // LANES, order * part, LANES), F32)] * 2,
        4 * order * moved.size,
        8 * moved.size,
    )(moved, kernel, outer, back)


def forward_mixed(first, grad_ret, kernel, gw, outer, back, members):
    order, part, channels = first.shape
    width = min(channels, 2 * LANES)
    local = order // members

    def body(f_ref, g_ref, k_ref, gw_ref, o_ref, b_ref, ret_ref, go_ref, gr_ref, held, held_g, result):
        @pl.when(pl.program_id(0) == 0)
        def _():
            go_ref[...] = jnp.zeros_like(go_ref)
            gr_ref[...] = jnp.zeros_like(gr_ref)

        spread(held, f_ref[...])
        spread(held_g, g_ref[...])
        for pair in tile_pairs(part, width):
            first_j = take(held, pair, order, part)
            mixed = dot(o_ref[...], first_j, (1, 0))
            weighted = (mixed * pick(k_ref, pair).astype(F32)).astype(BF16)
            put(result, pair, order, part, dot(b_ref[...], weighted, (1, 0)))
            go_ref[...] += dot(pick(gw_ref, pair), first_j, (1, 1))
            gr_ref[...] += dot(take(held_g, pair, order, part), weighted, (1, 1))
        ret_ref[...] = gather(result, members, part)

    moved = pl.BlockSpec((order, part, width), lambda g: (0, 0, g))
    mine = pl.BlockSpec((part, order, width), lambda g: (0, 0, g))
    small = (square(order), jax.ShapeDtypeStruct((order, order), F32))
    return call(
        body,
        (channels // width,),
        [moved, moved, mine, mine, square(order), square(order)],
        [
            (
                pl.BlockSpec((members, local, part, width), lambda g: (0, 0, 0, g)),
                jax.ShapeDtypeStruct((members, local, part, channels), BF16),
            ),
            small,
            small,
        ],
        [pltpu.VMEM((width // LANES, order * part, LANES), F32)] * 3,
        8 * order * first.size,
        10 * first.size,
    )(first, grad_ret, kernel, gw, outer, back)


def finish_values(grad_first, values, inner):
    members, rows, part, channels = grad_first.shape
    order = members * part
    step = max(1, rows // 2)

    def body(g_ref, v_ref, f_ref, gv_ref, gi_ref):
        @pl.when(pl.program_id(0) == 0)
        def _():
            gi_ref[...] = jnp.zeros_like(gi_ref)

        for r in range(step):
            g = g_ref[:, r].astype(F32).reshape(order, channels).astype(BF16)
            gv_ref[r] = dot(f_ref[...], g, (0, 0)).astype(BF16)
            gi_ref[...] += dot(g, v_ref[r], (1, 1))

    rowed = pl.BlockSpec((step, order, channels), lambda g: (g, 0, 0))
    return call(
        body,
        (rows // step,),
        [pl.BlockSpec((members, step, part, channels), lambda g: (0, g, 0, 0)), rowed, square(order)],
        [
            (rowed, jax.ShapeDtypeStruct(values.shape, BF16)),
            (square(order), jax.ShapeDtypeStruct((order, order), F32)),
        ],
        [],
        4 * order * values.size,
        6 * values.size,
    )(grad_first, values, inner)


def finish_return(returned, cotangent):
    members, rows, part, channels = returned.shape
    order = members * part
    step = max(1, rows // 2)
    steps = rows // step

    def body(r_ref, c_ref, o_ref, acc):
        @pl.when(pl.program_id(0) == 0)
        def _():
            acc[...] = jnp.zeros_like(acc)

        for r in range(step):
            ret = r_ref[:, r].astype(F32).reshape(order, channels).astype(BF16)
            acc[...] += dot(c_ref[r], ret, (1, 1))

        @pl.when(pl.program_id(0) == steps - 1)
        def _():
            o_ref[...] = acc[...].astype(BF16)

    return call(
        body,
        (steps,),
        [
            pl.BlockSpec((members, step, part, channels), lambda g: (0, g, 0, 0)),
            pl.BlockSpec((step, order, channels), lambda g: (g, 0, 0)),
        ],
        [(square(order), jax.ShapeDtypeStruct((order, order), BF16))],
        [pltpu.VMEM((order, order), F32)],
        2 * order * cotangent.size,
        4 * cotangent.size,
    )(returned, cotangent)[0]


def plain(values, kernel, cotangent, inner_factor, outer_factor, return_outer, return_inner):
    f32 = F32
    bf16 = BF16
    order_a = outer_factor.shape[0]
    order_b = inner_factor.shape[0]
    channels = kernel.shape[2]
    seq_count = values.shape[0] * lax.axis_size("dp")
    scale_a = 1.0 / math.sqrt(seq_count * order_a * channels)
    scale_b = 1.0 / math.sqrt(seq_count * order_b * channels)
    first = jnp.einsum("jb,sabc->sajc", inner_factor, values, preferred_element_type=f32).astype(
        bf16
    )
    piece = lax.all_to_all(first, "seq", split_axis=2, concat_axis=1, tiled=True)
    mixed = jnp.einsum("ia,sajc->sjic", outer_factor, piece, preferred_element_type=f32)
    first_moved = piece
    weighted = (mixed * kernel[None].astype(f32)).astype(bf16)
    returned_local = jnp.einsum(
        "ki,sjic->sjkc", return_outer, weighted, preferred_element_type=f32
    ).astype(bf16)
    returned = lax.all_to_all(returned_local, "seq", split_axis=2, concat_axis=1, tiled=True)
    grad_returned = jnp.einsum(
        "lj,sklc->skjc", return_inner, cotangent, preferred_element_type=f32
    ).astype(bf16)
    grad_gtwo = jnp.einsum("sklc,sjkc->lj", cotangent, returned, preferred_element_type=f32)
    piece = lax.all_to_all(grad_returned, "seq", split_axis=2, concat_axis=1, tiled=True)
    grad_mixed = jnp.einsum("ki,skjc->sjic", return_outer, piece, preferred_element_type=f32)
    grad_ret_moved = piece
    grad_gone = jnp.einsum("skjc,sjic->ki", grad_ret_moved, weighted, preferred_element_type=f32)
    grad_weighted = (grad_mixed * kernel[None].astype(f32)).astype(bf16)
    grad_first_moved = jnp.einsum(
        "ia,sjic->sajc", outer_factor, grad_weighted, preferred_element_type=f32
    ).astype(bf16)
    grad_ftwo = jnp.einsum("sjic,sajc->ia", grad_weighted, first_moved, preferred_element_type=f32)
    piece = lax.all_to_all(grad_first_moved, "seq", split_axis=1, concat_axis=2, tiled=True)
    grad_values = jnp.einsum(
        "jb,sajc->sabc", inner_factor, piece, preferred_element_type=f32
    ).astype(bf16)
    grad_fone = jnp.einsum("sajc,sabc->jb", piece, values, preferred_element_type=f32)
    summed = lax.psum((grad_fone, grad_ftwo, grad_gone, grad_gtwo), ("seq", "dp"))
    return (
        grad_values,
        summed[0] * scale_a,
        summed[1] * scale_b,
        summed[2] * scale_b,
        summed[3] * scale_a,
    )


def swap(x, bits):
    size = lax.axis_size("seq")
    return lax.ppermute(x, "seq", [(i, i ^ bits) for i in range(size)])


def move(x):
    return lax.all_to_all(x, "seq", 0, 0, tiled=True)


def halves(x, bit):
    mine = (lax.axis_index("seq") // bit) % 2
    pair = x.reshape(2, x.shape[0] // 2, x.shape[1])
    return (
        lax.dynamic_index_in_dim(pair, mine, 0, keepdims=False),
        lax.dynamic_index_in_dim(pair, 1 - mine, 0, keepdims=False),
    )


def join(mine, other, bit):
    first = (lax.axis_index("seq") // bit) % 2 == 0
    return jnp.concatenate((jnp.where(first, mine, other), jnp.where(first, other, mine)), axis=0)


def plane_sum(x):
    for bit in (1, 2, 4):
        keep, give = halves(x, bit)
        x = keep + swap(give, bit)
    return x


def across(x):
    x = x.astype(BF16)
    near, *far = [swap(x, bits) for bits in (8, 16, 24)]
    return x, near, *far


def joined(x):
    for bit in (4, 2, 1):
        x = join(x, swap(x, bit), bit)
    return x


def late_sum(x):
    size = lax.axis_size("seq")
    rows, columns = x.shape
    parts = move(x.reshape(size, rows // size, columns))
    held = jnp.sum(parts.astype(F32), axis=0).astype(BF16)
    return move(jnp.broadcast_to(held[None], parts.shape)).reshape(rows, columns).astype(F32)


def per_device(values, kernel, cotangent, inner_factor, outer_factor, return_outer, return_inner):
    members = lax.axis_size("seq")
    order = outer_factor.shape[0]
    rows, channels = kernel.shape[0], kernel.shape[2]
    if (
        members != 32
        or lax.axis_size("dp") != 1
        or values.shape[0] != 1
        or rows != 8
        or inner_factor.shape[0] != order
        or channels % (2 * LANES)
    ):
        return plain(
            values, kernel, cotangent, inner_factor, outer_factor, return_outer, return_inner
        )
    scale = 1.0 / math.sqrt(order * channels)

    grad_ret = move(apply_inner(cotangent[0], return_inner, 0, members))
    sent = apply_inner(values[0], inner_factor, 1, members)
    sent, grad_ret = lax.optimization_barrier((sent, grad_ret))
    first = move(sent)
    grad_ret = grad_ret.reshape(order, rows, channels)
    gw, sent = backward_mixed(grad_ret, kernel, outer_factor, return_outer, members)
    sent, first = lax.optimization_barrier((sent, first))
    grad_first = move(sent)
    first = first.reshape(order, rows, channels)
    sent, grad_outer, grad_back = forward_mixed(
        first, grad_ret, kernel, gw, outer_factor, return_outer, members
    )
    sent, grad_first = lax.optimization_barrier((sent, grad_first))
    returned = move(sent)
    grad_values, grad_inner = finish_values(grad_first, values[0], inner_factor)
    early = plane_sum(jnp.concatenate((grad_inner, grad_outer, grad_back), axis=1))
    quarters = across(early)
    grad_last = finish_return(returned, cotangent[0])
    (a, b, c, d), grad_last = lax.optimization_barrier((quarters, grad_last))
    early = (a.astype(F32) + b.astype(F32)) + (c.astype(F32) + d.astype(F32))
    early = joined(early) * scale
    grad_last = late_sum(grad_last) * scale
    return (grad_values[None], *jnp.split(early, 3, axis=1), grad_last)


def solution(mesh):
    return jax.shard_map(
        per_device,
        mesh=mesh,
        in_specs=(
            P(("groups", "dp"), "seq", None, None),
            P("seq", None, None),
            P(("groups", "dp"), "seq", None, None),
            P(),
            P(),
            P(),
            P(),
        ),
        out_specs=(
            P(("groups", "dp"), "seq", None, None),
            P("groups", None),
            P("groups", None),
            P("groups", None),
            P("groups", None),
        ),
        check_vma=False,
    )
```

```python
import math

import jax
import jax.numpy as jnp
from jax import lax
from jax.experimental import pallas as pl
from jax.experimental.pallas import tpu as pltpu
from jax.sharding import PartitionSpec as P

F32 = jnp.float32
BF16 = jnp.bfloat16
LANES = 128
VMEM = 63 * 2**20


def dot(x, y, dims):
    return lax.dot_general(x, y, ((dims[:1], dims[1:]), ((), ())), preferred_element_type=F32)


def call(body, grid, ins, outs, scratch, flops, moved):
    return pl.pallas_call(
        body,
        grid=grid,
        in_specs=[spec for spec in ins],
        out_specs=[spec for spec, _ in outs],
        out_shape=[shape for _, shape in outs],
        scratch_shapes=scratch,
        compiler_params=pltpu.CompilerParams(
            vmem_limit_bytes=VMEM, dimension_semantics=("arbitrary",) * len(grid)
        ),
        cost_estimate=pl.CostEstimate(flops=flops, bytes_accessed=moved, transcendentals=0),
    )


def square(order):
    return pl.BlockSpec((order, order), lambda *g: (0, 0))


def apply_inner(x, factor, side, members):
    rows, order, channels = x.shape
    part = order // members
    step = max(1, rows // 2)

    def body(x_ref, f_ref, o_ref):
        for r in range(step):
            y = dot(f_ref[...], x_ref[r], (side, 0))
            o_ref[:, r] = y.reshape(members, part, channels).astype(BF16)

    return call(
        body,
        (rows // step,),
        [pl.BlockSpec((step, order, channels), lambda g: (g, 0, 0)), square(order)],
        [
            (
                pl.BlockSpec((members, step, part, channels), lambda g: (0, g, 0, 0)),
                jax.ShapeDtypeStruct((members, rows, part, channels), BF16),
            )
        ],
        [],
        2 * order * x.size,
        4 * x.size,
    )(x, factor)[0]


def tile_pairs(part, width):
    tiles = [(j, t) for j in range(part) for t in range(width // LANES)]
    return [tiles[p : p + 2] for p in range(0, len(tiles), 2)]


def spread(ref, value):
    order, part, width = value.shape
    for t in range(width // LANES):
        ref[t] = value[:, :, t * LANES : (t + 1) * LANES].astype(F32).reshape(order * part, LANES)


def take(ref, pair, order, part):
    got = [ref[t, pl.ds(j, order, stride=part), :] for j, t in pair]
    return jnp.concatenate(got, axis=1).astype(BF16)


def put(ref, pair, order, part, value):
    for n, (j, t) in enumerate(pair):
        ref[t, pl.ds(j, order, stride=part), :] = value[:, n * LANES : (n + 1) * LANES]


def gather(ref, members, part):
    tiles = [ref[t].reshape(members, -1, part, LANES).astype(BF16) for t in range(ref.shape[0])]
    return jnp.concatenate(tiles, axis=-1)


def pick(ref, pair):
    return jnp.concatenate([ref[j, :, t * LANES : (t + 1) * LANES] for j, t in pair], axis=1)


def backward_mixed(moved, kernel, outer, back, members):
    order, part, channels = moved.shape
    width = min(channels, 2 * LANES)
    local = order // members

    def body(m_ref, k_ref, o_ref, b_ref, gw_ref, gf_ref, held, result):
        spread(held, m_ref[...])
        for pair in tile_pairs(part, width):
            mixed = dot(b_ref[...], take(held, pair, order, part), (0, 0))
            gw = (mixed * pick(k_ref, pair).astype(F32)).astype(BF16)
            for n, (j, t) in enumerate(pair):
                gw_ref[j, :, t * LANES : (t + 1) * LANES] = gw[:, n * LANES : (n + 1) * LANES]
            put(result, pair, order, part, dot(o_ref[...], gw, (0, 0)))
        gf_ref[...] = gather(result, members, part)

    return call(
        body,
        (channels // width,),
        [
            pl.BlockSpec((order, part, width), lambda g: (0, 0, g)),
            pl.BlockSpec((part, order, width), lambda g: (0, 0, g)),
            square(order),
            square(order),
        ],
        [
            (
                pl.BlockSpec((part, order, width), lambda g: (0, 0, g)),
                jax.ShapeDtypeStruct((part, order, channels), BF16),
            ),
            (
                pl.BlockSpec((members, local, part, width), lambda g: (0, 0, 0, g)),
                jax.ShapeDtypeStruct((members, local, part, channels), BF16),
            ),
        ],
        [pltpu.VMEM((width // LANES, order * part, LANES), F32)] * 2,
        4 * order * moved.size,
        8 * moved.size,
    )(moved, kernel, outer, back)


def forward_mixed(first, grad_ret, kernel, gw, outer, back, members):
    order, part, channels = first.shape
    width = min(channels, 2 * LANES)
    local = order // members

    def body(f_ref, g_ref, k_ref, gw_ref, o_ref, b_ref, ret_ref, go_ref, gr_ref, held, held_g, result):
        @pl.when(pl.program_id(0) == 0)
        def _():
            go_ref[...] = jnp.zeros_like(go_ref)
            gr_ref[...] = jnp.zeros_like(gr_ref)

        spread(held, f_ref[...])
        spread(held_g, g_ref[...])
        for pair in tile_pairs(part, width):
            first_j = take(held, pair, order, part)
            mixed = dot(o_ref[...], first_j, (1, 0))
            weighted = (mixed * pick(k_ref, pair).astype(F32)).astype(BF16)
            put(result, pair, order, part, dot(b_ref[...], weighted, (1, 0)))
            go_ref[...] += dot(pick(gw_ref, pair), first_j, (1, 1))
            gr_ref[...] += dot(take(held_g, pair, order, part), weighted, (1, 1))
        ret_ref[...] = gather(result, members, part)

    moved = pl.BlockSpec((order, part, width), lambda g: (0, 0, g))
    mine = pl.BlockSpec((part, order, width), lambda g: (0, 0, g))
    small = (square(order), jax.ShapeDtypeStruct((order, order), F32))
    return call(
        body,
        (channels // width,),
        [moved, moved, mine, mine, square(order), square(order)],
        [
            (
                pl.BlockSpec((members, local, part, width), lambda g: (0, 0, 0, g)),
                jax.ShapeDtypeStruct((members, local, part, channels), BF16),
            ),
            small,
            small,
        ],
        [pltpu.VMEM((width // LANES, order * part, LANES), F32)] * 3,
        8 * order * first.size,
        10 * first.size,
    )(first, grad_ret, kernel, gw, outer, back)


def finish_values(grad_first, values, inner):
    members, rows, part, channels = grad_first.shape
    order = members * part
    step = max(1, rows // 2)

    def body(g_ref, v_ref, f_ref, gv_ref, gi_ref):
        @pl.when(pl.program_id(0) == 0)
        def _():
            gi_ref[...] = jnp.zeros_like(gi_ref)

        for r in range(step):
            g = g_ref[:, r].astype(F32).reshape(order, channels).astype(BF16)
            gv_ref[r] = dot(f_ref[...], g, (0, 0)).astype(BF16)
            gi_ref[...] += dot(g, v_ref[r], (1, 1))

    rowed = pl.BlockSpec((step, order, channels), lambda g: (g, 0, 0))
    return call(
        body,
        (rows // step,),
        [pl.BlockSpec((members, step, part, channels), lambda g: (0, g, 0, 0)), rowed, square(order)],
        [
            (rowed, jax.ShapeDtypeStruct(values.shape, BF16)),
            (square(order), jax.ShapeDtypeStruct((order, order), F32)),
        ],
        [],
        4 * order * values.size,
        6 * values.size,
    )(grad_first, values, inner)


def finish_return(returned, cotangent):
    members, rows, part, channels = returned.shape
    order = members * part
    step = max(1, rows // 2)
    steps = rows // step

    def body(r_ref, c_ref, o_ref, acc):
        @pl.when(pl.program_id(0) == 0)
        def _():
            acc[...] = jnp.zeros_like(acc)

        for r in range(step):
            ret = r_ref[:, r].astype(F32).reshape(order, channels).astype(BF16)
            acc[...] += dot(c_ref[r], ret, (1, 1))

        @pl.when(pl.program_id(0) == steps - 1)
        def _():
            o_ref[...] = acc[...].astype(BF16)

    return call(
        body,
        (steps,),
        [
            pl.BlockSpec((members, step, part, channels), lambda g: (0, g, 0, 0)),
            pl.BlockSpec((step, order, channels), lambda g: (g, 0, 0)),
        ],
        [(square(order), jax.ShapeDtypeStruct((order, order), BF16))],
        [pltpu.VMEM((order, order), F32)],
        2 * order * cotangent.size,
        4 * cotangent.size,
    )(returned, cotangent)[0]


def plain(values, kernel, cotangent, inner_factor, outer_factor, return_outer, return_inner):
    f32 = F32
    bf16 = BF16
    order_a = outer_factor.shape[0]
    order_b = inner_factor.shape[0]
    channels = kernel.shape[2]
    seq_count = values.shape[0] * lax.axis_size("dp")
    scale_a = 1.0 / math.sqrt(seq_count * order_a * channels)
    scale_b = 1.0 / math.sqrt(seq_count * order_b * channels)
    first = jnp.einsum("jb,sabc->sajc", inner_factor, values, preferred_element_type=f32).astype(
        bf16
    )
    piece = lax.all_to_all(first, "seq", split_axis=2, concat_axis=1, tiled=True)
    mixed = jnp.einsum("ia,sajc->sjic", outer_factor, piece, preferred_element_type=f32)
    first_moved = piece
    weighted = (mixed * kernel[None].astype(f32)).astype(bf16)
    returned_local = jnp.einsum(
        "ki,sjic->sjkc", return_outer, weighted, preferred_element_type=f32
    ).astype(bf16)
    returned = lax.all_to_all(returned_local, "seq", split_axis=2, concat_axis=1, tiled=True)
    grad_returned = jnp.einsum(
        "lj,sklc->skjc", return_inner, cotangent, preferred_element_type=f32
    ).astype(bf16)
    grad_gtwo = jnp.einsum("sklc,sjkc->lj", cotangent, returned, preferred_element_type=f32)
    piece = lax.all_to_all(grad_returned, "seq", split_axis=2, concat_axis=1, tiled=True)
    grad_mixed = jnp.einsum("ki,skjc->sjic", return_outer, piece, preferred_element_type=f32)
    grad_ret_moved = piece
    grad_gone = jnp.einsum("skjc,sjic->ki", grad_ret_moved, weighted, preferred_element_type=f32)
    grad_weighted = (grad_mixed * kernel[None].astype(f32)).astype(bf16)
    grad_first_moved = jnp.einsum(
        "ia,sjic->sajc", outer_factor, grad_weighted, preferred_element_type=f32
    ).astype(bf16)
    grad_ftwo = jnp.einsum("sjic,sajc->ia", grad_weighted, first_moved, preferred_element_type=f32)
    piece = lax.all_to_all(grad_first_moved, "seq", split_axis=1, concat_axis=2, tiled=True)
    grad_values = jnp.einsum(
        "jb,sajc->sabc", inner_factor, piece, preferred_element_type=f32
    ).astype(bf16)
    grad_fone = jnp.einsum("sajc,sabc->jb", piece, values, preferred_element_type=f32)
    summed = lax.psum((grad_fone, grad_ftwo, grad_gone, grad_gtwo), ("seq", "dp"))
    return (
        grad_values,
        summed[0] * scale_a,
        summed[1] * scale_b,
        summed[2] * scale_b,
        summed[3] * scale_a,
    )


def swap(x, bits):
    size = lax.axis_size("seq")
    return lax.ppermute(x, "seq", [(i, i ^ bits) for i in range(size)])


def move(x):
    return lax.all_to_all(x, "seq", 0, 0, tiled=True)


def halves(x, bit):
    mine = (lax.axis_index("seq") // bit) % 2
    pair = x.reshape(2, x.shape[0] // 2, x.shape[1])
    return (
        lax.dynamic_index_in_dim(pair, mine, 0, keepdims=False),
        lax.dynamic_index_in_dim(pair, 1 - mine, 0, keepdims=False),
    )


def join(mine, other, bit):
    first = (lax.axis_index("seq") // bit) % 2 == 0
    return jnp.concatenate((jnp.where(first, mine, other), jnp.where(first, other, mine)), axis=0)


def plane_sum(x):
    for bit in (1, 2, 4):
        keep, give = halves(x, bit)
        x = keep + swap(give, bit)
    return x


def joined(x):
    for bit in (4, 2, 1):
        x = join(x, swap(x, bit), bit)
    return x


def late_sum(x):
    size = lax.axis_size("seq")
    rows, columns = x.shape
    parts = move(x.reshape(size, rows // size, columns))
    held = jnp.sum(parts.astype(F32), axis=0).astype(BF16)
    return move(jnp.broadcast_to(held[None], parts.shape)).reshape(rows, columns).astype(F32)


def per_device(values, kernel, cotangent, inner_factor, outer_factor, return_outer, return_inner):
    members = lax.axis_size("seq")
    order = outer_factor.shape[0]
    rows, channels = kernel.shape[0], kernel.shape[2]
    if (
        members != 32
        or lax.axis_size("dp") != 1
        or values.shape[0] != 1
        or rows != 8
        or inner_factor.shape[0] != order
        or channels % (2 * LANES)
    ):
        return plain(
            values, kernel, cotangent, inner_factor, outer_factor, return_outer, return_inner
        )
    scale = 1.0 / math.sqrt(order * channels)

    grad_ret = move(apply_inner(cotangent[0], return_inner, 0, members))
    sent = apply_inner(values[0], inner_factor, 1, members)
    sent, grad_ret = lax.optimization_barrier((sent, grad_ret))
    first = move(sent)
    grad_ret = grad_ret.reshape(order, rows, channels)
    gw, sent = backward_mixed(grad_ret, kernel, outer_factor, return_outer, members)
    sent, first = lax.optimization_barrier((sent, first))
    grad_first = move(sent)
    first = first.reshape(order, rows, channels)
    sent, grad_outer, grad_back = forward_mixed(
        first, grad_ret, kernel, gw, outer_factor, return_outer, members
    )
    sent, grad_first = lax.optimization_barrier((sent, grad_first))
    returned = move(sent)
    grad_values, grad_inner = finish_values(grad_first, values[0], inner_factor)
    early = plane_sum(jnp.concatenate((grad_inner, grad_outer, grad_back), axis=1))
    early = early + swap(early, 8)
    returned, early = lax.optimization_barrier((returned, early))
    early = early.astype(BF16)
    other = swap(early, 16)
    grad_last = finish_return(returned, cotangent[0])
    other, grad_last = lax.optimization_barrier((other, grad_last))
    early = early.astype(F32) + other.astype(F32)
    early = joined(early) * scale
    grad_last = late_sum(grad_last) * scale
    return (grad_values[None], *jnp.split(early, 3, axis=1), grad_last)


def solution(mesh):
    return jax.shard_map(
        per_device,
        mesh=mesh,
        in_specs=(
            P(("groups", "dp"), "seq", None, None),
            P("seq", None, None),
            P(("groups", "dp"), "seq", None, None),
            P(),
            P(),
            P(),
            P(),
        ),
        out_specs=(
            P(("groups", "dp"), "seq", None, None),
            P("groups", None),
            P("groups", None),
            P("groups", None),
            P("groups", None),
        ),
        check_vma=False,
    )
```

```python
import math

import jax
import jax.numpy as jnp
from jax import lax
from jax.experimental import pallas as pl
from jax.experimental.pallas import tpu as pltpu
from jax.sharding import PartitionSpec as P

F32 = jnp.float32
BF16 = jnp.bfloat16
LANES = 128
VMEM = 63 * 2**20


def dot(x, y, dims):
    return lax.dot_general(x, y, ((dims[:1], dims[1:]), ((), ())), preferred_element_type=F32)


def call(body, grid, ins, outs, scratch, flops, moved):
    return pl.pallas_call(
        body,
        grid=grid,
        in_specs=[spec for spec in ins],
        out_specs=[spec for spec, _ in outs],
        out_shape=[shape for _, shape in outs],
        scratch_shapes=scratch,
        compiler_params=pltpu.CompilerParams(
            vmem_limit_bytes=VMEM, dimension_semantics=("arbitrary",) * len(grid)
        ),
        cost_estimate=pl.CostEstimate(flops=flops, bytes_accessed=moved, transcendentals=0),
    )


def square(order):
    return pl.BlockSpec((order, order), lambda *g: (0, 0))


def apply_inner(x, factor, side, members):
    rows, order, channels = x.shape
    part = order // members
    step = max(1, rows // 2)

    def body(x_ref, f_ref, o_ref):
        for r in range(step):
            y = dot(f_ref[...], x_ref[r], (side, 0))
            o_ref[:, r] = y.reshape(members, part, channels).astype(BF16)

    return call(
        body,
        (rows // step,),
        [pl.BlockSpec((step, order, channels), lambda g: (g, 0, 0)), square(order)],
        [
            (
                pl.BlockSpec((members, step, part, channels), lambda g: (0, g, 0, 0)),
                jax.ShapeDtypeStruct((members, rows, part, channels), BF16),
            )
        ],
        [],
        2 * order * x.size,
        4 * x.size,
    )(x, factor)[0]


def tile_pairs(part, width):
    tiles = [(j, t) for j in range(part) for t in range(width // LANES)]
    return [tiles[p : p + 2] for p in range(0, len(tiles), 2)]


def spread(ref, value):
    order, part, width = value.shape
    for t in range(width // LANES):
        ref[t] = value[:, :, t * LANES : (t + 1) * LANES].astype(F32).reshape(order * part, LANES)


def take(ref, pair, order, part):
    got = [ref[t, pl.ds(j, order, stride=part), :] for j, t in pair]
    return jnp.concatenate(got, axis=1).astype(BF16)


def put(ref, pair, order, part, value):
    for n, (j, t) in enumerate(pair):
        ref[t, pl.ds(j, order, stride=part), :] = value[:, n * LANES : (n + 1) * LANES]


def gather(ref, members, part):
    tiles = [ref[t].reshape(members, -1, part, LANES).astype(BF16) for t in range(ref.shape[0])]
    return jnp.concatenate(tiles, axis=-1)


def pick(ref, pair):
    return jnp.concatenate([ref[j, :, t * LANES : (t + 1) * LANES] for j, t in pair], axis=1)


def backward_mixed(moved, kernel, outer, back, members):
    order, part, channels = moved.shape
    width = min(channels, 2 * LANES)
    local = order // members

    def body(m_ref, k_ref, o_ref, b_ref, gw_ref, gf_ref, held, result):
        spread(held, m_ref[...])
        for pair in tile_pairs(part, width):
            mixed = dot(b_ref[...], take(held, pair, order, part), (0, 0))
            gw = (mixed * pick(k_ref, pair).astype(F32)).astype(BF16)
            for n, (j, t) in enumerate(pair):
                gw_ref[j, :, t * LANES : (t + 1) * LANES] = gw[:, n * LANES : (n + 1) * LANES]
            put(result, pair, order, part, dot(o_ref[...], gw, (0, 0)))
        gf_ref[...] = gather(result, members, part)

    return call(
        body,
        (channels // width,),
        [
            pl.BlockSpec((order, part, width), lambda g: (0, 0, g)),
            pl.BlockSpec((part, order, width), lambda g: (0, 0, g)),
            square(order),
            square(order),
        ],
        [
            (
                pl.BlockSpec((part, order, width), lambda g: (0, 0, g)),
                jax.ShapeDtypeStruct((part, order, channels), BF16),
            ),
            (
                pl.BlockSpec((members, local, part, width), lambda g: (0, 0, 0, g)),
                jax.ShapeDtypeStruct((members, local, part, channels), BF16),
            ),
        ],
        [pltpu.VMEM((width // LANES, order * part, LANES), F32)] * 2,
        4 * order * moved.size,
        8 * moved.size,
    )(moved, kernel, outer, back)


def forward_mixed(first, grad_ret, kernel, gw, outer, back, members):
    order, part, channels = first.shape
    width = min(channels, 2 * LANES)
    local = order // members

    def body(f_ref, g_ref, k_ref, gw_ref, o_ref, b_ref, ret_ref, go_ref, gr_ref, held, held_g, result):
        @pl.when(pl.program_id(0) == 0)
        def _():
            go_ref[...] = jnp.zeros_like(go_ref)
            gr_ref[...] = jnp.zeros_like(gr_ref)

        spread(held, f_ref[...])
        spread(held_g, g_ref[...])
        for pair in tile_pairs(part, width):
            first_j = take(held, pair, order, part)
            mixed = dot(o_ref[...], first_j, (1, 0))
            weighted = (mixed * pick(k_ref, pair).astype(F32)).astype(BF16)
            put(result, pair, order, part, dot(b_ref[...], weighted, (1, 0)))
            go_ref[...] += dot(pick(gw_ref, pair), first_j, (1, 1))
            gr_ref[...] += dot(take(held_g, pair, order, part), weighted, (1, 1))
        ret_ref[...] = gather(result, members, part)

    moved = pl.BlockSpec((order, part, width), lambda g: (0, 0, g))
    mine = pl.BlockSpec((part, order, width), lambda g: (0, 0, g))
    small = (square(order), jax.ShapeDtypeStruct((order, order), F32))
    return call(
        body,
        (channels // width,),
        [moved, moved, mine, mine, square(order), square(order)],
        [
            (
                pl.BlockSpec((members, local, part, width), lambda g: (0, 0, 0, g)),
                jax.ShapeDtypeStruct((members, local, part, channels), BF16),
            ),
            small,
            small,
        ],
        [pltpu.VMEM((width // LANES, order * part, LANES), F32)] * 3,
        8 * order * first.size,
        10 * first.size,
    )(first, grad_ret, kernel, gw, outer, back)


def finish_values(grad_first, values, inner):
    members, rows, part, channels = grad_first.shape
    order = members * part
    step = max(1, rows // 2)

    def body(g_ref, v_ref, f_ref, gv_ref, gi_ref):
        @pl.when(pl.program_id(0) == 0)
        def _():
            gi_ref[...] = jnp.zeros_like(gi_ref)

        for r in range(step):
            g = g_ref[:, r].astype(F32).reshape(order, channels).astype(BF16)
            gv_ref[r] = dot(f_ref[...], g, (0, 0)).astype(BF16)
            gi_ref[...] += dot(g, v_ref[r], (1, 1))

    rowed = pl.BlockSpec((step, order, channels), lambda g: (g, 0, 0))
    return call(
        body,
        (rows // step,),
        [pl.BlockSpec((members, step, part, channels), lambda g: (0, g, 0, 0)), rowed, square(order)],
        [
            (rowed, jax.ShapeDtypeStruct(values.shape, BF16)),
            (square(order), jax.ShapeDtypeStruct((order, order), F32)),
        ],
        [],
        4 * order * values.size,
        6 * values.size,
    )(grad_first, values, inner)


def finish_return(returned, cotangent):
    members, rows, part, channels = returned.shape
    order = members * part

    def body(r_ref, c_ref, o_ref):
        acc = jnp.zeros((order, order), F32)
        for r in range(rows):
            ret = r_ref[:, r].astype(F32).reshape(order, channels).astype(BF16)
            acc += dot(c_ref[r], ret, (1, 1))
        o_ref[...] = acc.astype(BF16)

    whole = pl.BlockSpec(memory_space=pltpu.VMEM)
    return pl.pallas_call(
        body,
        in_specs=[whole, whole],
        out_specs=whole,
        out_shape=jax.ShapeDtypeStruct((order, order), BF16),
        compiler_params=pltpu.CompilerParams(vmem_limit_bytes=24 * 2**20),
        cost_estimate=pl.CostEstimate(
            flops=2 * order * cotangent.size, bytes_accessed=4 * cotangent.size, transcendentals=0
        ),
    )(returned, cotangent)


def plain(values, kernel, cotangent, inner_factor, outer_factor, return_outer, return_inner):
    f32 = F32
    bf16 = BF16
    order_a = outer_factor.shape[0]
    order_b = inner_factor.shape[0]
    channels = kernel.shape[2]
    seq_count = values.shape[0] * lax.axis_size("dp")
    scale_a = 1.0 / math.sqrt(seq_count * order_a * channels)
    scale_b = 1.0 / math.sqrt(seq_count * order_b * channels)
    first = jnp.einsum("jb,sabc->sajc", inner_factor, values, preferred_element_type=f32).astype(
        bf16
    )
    piece = lax.all_to_all(first, "seq", split_axis=2, concat_axis=1, tiled=True)
    mixed = jnp.einsum("ia,sajc->sjic", outer_factor, piece, preferred_element_type=f32)
    first_moved = piece
    weighted = (mixed * kernel[None].astype(f32)).astype(bf16)
    returned_local = jnp.einsum(
        "ki,sjic->sjkc", return_outer, weighted, preferred_element_type=f32
    ).astype(bf16)
    returned = lax.all_to_all(returned_local, "seq", split_axis=2, concat_axis=1, tiled=True)
    grad_returned = jnp.einsum(
        "lj,sklc->skjc", return_inner, cotangent, preferred_element_type=f32
    ).astype(bf16)
    grad_gtwo = jnp.einsum("sklc,sjkc->lj", cotangent, returned, preferred_element_type=f32)
    piece = lax.all_to_all(grad_returned, "seq", split_axis=2, concat_axis=1, tiled=True)
    grad_mixed = jnp.einsum("ki,skjc->sjic", return_outer, piece, preferred_element_type=f32)
    grad_ret_moved = piece
    grad_gone = jnp.einsum("skjc,sjic->ki", grad_ret_moved, weighted, preferred_element_type=f32)
    grad_weighted = (grad_mixed * kernel[None].astype(f32)).astype(bf16)
    grad_first_moved = jnp.einsum(
        "ia,sjic->sajc", outer_factor, grad_weighted, preferred_element_type=f32
    ).astype(bf16)
    grad_ftwo = jnp.einsum("sjic,sajc->ia", grad_weighted, first_moved, preferred_element_type=f32)
    piece = lax.all_to_all(grad_first_moved, "seq", split_axis=1, concat_axis=2, tiled=True)
    grad_values = jnp.einsum(
        "jb,sajc->sabc", inner_factor, piece, preferred_element_type=f32
    ).astype(bf16)
    grad_fone = jnp.einsum("sajc,sabc->jb", piece, values, preferred_element_type=f32)
    summed = lax.psum((grad_fone, grad_ftwo, grad_gone, grad_gtwo), ("seq", "dp"))
    return (
        grad_values,
        summed[0] * scale_a,
        summed[1] * scale_b,
        summed[2] * scale_b,
        summed[3] * scale_a,
    )


def swap(x, bits):
    size = lax.axis_size("seq")
    return lax.ppermute(x, "seq", [(i, i ^ bits) for i in range(size)])


def move(x):
    return lax.all_to_all(x, "seq", 0, 0, tiled=True)


def halves(x, bit):
    mine = (lax.axis_index("seq") // bit) % 2
    pair = x.reshape(2, x.shape[0] // 2, x.shape[1])
    return (
        lax.dynamic_index_in_dim(pair, mine, 0, keepdims=False),
        lax.dynamic_index_in_dim(pair, 1 - mine, 0, keepdims=False),
    )


def join(mine, other, bit):
    first = (lax.axis_index("seq") // bit) % 2 == 0
    return jnp.concatenate((jnp.where(first, mine, other), jnp.where(first, other, mine)), axis=0)


def plane_sum(x):
    for bit in (1, 2, 4):
        keep, give = halves(x, bit)
        x = keep + swap(give, bit)
    return x


def joined(x):
    for bit in (4, 2, 1):
        x = join(x, swap(x, bit), bit)
    return x


def late_sum(x):
    size = lax.axis_size("seq")
    rows, columns = x.shape
    parts = move(x.reshape(size, rows // size, columns))
    held = jnp.sum(parts.astype(F32), axis=0).astype(BF16)
    return move(jnp.broadcast_to(held[None], parts.shape)).reshape(rows, columns).astype(F32)


def per_device(values, kernel, cotangent, inner_factor, outer_factor, return_outer, return_inner):
    members = lax.axis_size("seq")
    order = outer_factor.shape[0]
    rows, channels = kernel.shape[0], kernel.shape[2]
    if (
        members != 32
        or lax.axis_size("dp") != 1
        or values.shape[0] != 1
        or rows != 8
        or inner_factor.shape[0] != order
        or channels % (2 * LANES)
    ):
        return plain(
            values, kernel, cotangent, inner_factor, outer_factor, return_outer, return_inner
        )
    scale = 1.0 / math.sqrt(order * channels)

    grad_ret = move(apply_inner(cotangent[0], return_inner, 0, members))
    sent = apply_inner(values[0], inner_factor, 1, members)
    sent, grad_ret = lax.optimization_barrier((sent, grad_ret))
    first = move(sent)
    grad_ret = grad_ret.reshape(order, rows, channels)
    gw, sent = backward_mixed(grad_ret, kernel, outer_factor, return_outer, members)
    sent, first = lax.optimization_barrier((sent, first))
    grad_first = move(sent)
    first = first.reshape(order, rows, channels)
    sent, grad_outer, grad_back = forward_mixed(
        first, grad_ret, kernel, gw, outer_factor, return_outer, members
    )
    sent, grad_first = lax.optimization_barrier((sent, grad_first))
    returned = move(sent)
    grad_values, grad_inner = finish_values(grad_first, values[0], inner_factor)
    early = plane_sum(jnp.concatenate((grad_inner, grad_outer, grad_back), axis=1))
    early = early + swap(early, 8)
    early = early.astype(BF16)
    other = swap(early, 16)
    grad_last = finish_return(returned, cotangent[0])
    other, grad_last = lax.optimization_barrier((other, grad_last))
    early = early.astype(F32) + other.astype(F32)
    early = joined(early) * scale
    grad_last = late_sum(grad_last) * scale
    return (grad_values[None], *jnp.split(early, 3, axis=1), grad_last)


def solution(mesh):
    return jax.shard_map(
        per_device,
        mesh=mesh,
        in_specs=(
            P(("groups", "dp"), "seq", None, None),
            P("seq", None, None),
            P(("groups", "dp"), "seq", None, None),
            P(),
            P(),
            P(),
            P(),
        ),
        out_specs=(
            P(("groups", "dp"), "seq", None, None),
            P("groups", None),
            P("groups", None),
            P("groups", None),
            P("groups", None),
        ),
        check_vma=False,
    )
```
